256 devices in a mesh: expert: 4 (over z_lo, core), fsdp: 64 (over x, y, z_hi).
Axes of the slice: x: 4, y: 4, z: 8 (z_hi: 4, z_lo: 2; z = z_hi * 2 + z_lo), core: 2. Of those that a mesh axis runs over, the one named last changes fastest.
Arguments:
- tokens: bfloat16 [512, 4096], P(('expert', 'fsdp')), may hold values from -6 to 6
- routes: int32 [512, 2], P(('expert', 'fsdp')), may hold values from 0 to 3, all different within a row; in each aligned block of 2 rows (0 to 1, 2 to 3, ...) at most 2 rows name the same one
- gates: float32 [512, 2], P(('expert', 'fsdp')), may hold values from 0.2 to 1
- out_grad: bfloat16 [512, 4096], P(('expert', 'fsdp')), may hold values from -6 to 6
- gate_weight: bfloat16 [4, 4096, 16384], P('expert', None, 'fsdp'), may hold values from -0.09375 to 0.09375
- up_weight: bfloat16 [4, 4096, 16384], P('expert', None, 'fsdp'), may hold values from -0.09375 to 0.09375
- down_weight: bfloat16 [4, 16384, 4096], P('expert', 'fsdp'), may hold values from -0.046875 to 0.046875
Outputs:
- tokens_grad: bfloat16 [512, 4096], P(('expert', 'fsdp'))
- gate_weight_grad: bfloat16 [4, 4096, 16384], P('expert', None, 'fsdp')
- up_weight_grad: bfloat16 [4, 4096, 16384], P('expert', None, 'fsdp')
- down_weight_grad: bfloat16 [4, 16384, 4096], P('expert', 'fsdp')
The draws below stay inside these ranges and needn't reach their ends.
Inputs may be any that keep to these rules, and one draw needn't show every extreme that they name: `routes`: each token names two different experts. The 2 tokens of one device name one expert at most 2 times, and in every draw some device's tokens name some expert exactly 2 times.
All inputs are finite; a program needn't handle non-finite values.
Results may differ from the reference program's by a relative error of at most 0.0066.
Values may be sent and summed in bfloat16 or wider, within the bound.
A program may use at most 128 MiB of HBM per device.

```python
import math
import jax
import jax.numpy as jnp
import numpy as np
from jax import lax

D = 4096
FF = 16384
TOK_DEV = 2
MOST = 2
EXPERTS = 4
TOKENS = 512
N_EXPERT = 4
N_FSDP = 64


def levels(own_key, dims, pieces, least, high):
    def one(dim, parts):
        draws = jax.random.uniform(jax.random.fold_in(jax.random.fold_in(own_key, 6), dim), (parts,), jnp.float32, least / len(pieces), high / len(pieces))
        return jnp.repeat(jnp.exp(draws), dims[dim] // parts).reshape((-1,) + (1,) * (len(dims) - dim - 1))

    loudness = one(*pieces[0])
    for cut in pieces[1:]:
        loudness = loudness * one(*cut)
    return loudness


def assign_block(own_key, own, number, rows, number_of, top, limit, lean):
    order = jax.random.permutation(own_key, number_of)
    packed, ordinary = portions_of(number_of, rows * top, limit, lean, True), portions_of(number_of, rows * top, limit, lean, False)
    places = jnp.arange(number_of)

    def named(tallies, rotation):
        used = int((tallies > 0).sum())
        fixed = max(1, used // 4)
        shifted = fixed + (places - fixed + rotation * (used - fixed)) % max(1, number_of - fixed)
        return jnp.zeros((number_of,), jnp.int32).at[order[jnp.where(places < fixed, places, shifted)]].set(jnp.asarray(tallies, jnp.int32))

    tallies = jnp.where(number % 4 == 0, named(packed, number // 4), named(ordinary, number - number // 4 - 1))
    mixed = jax.random.permutation(jax.random.fold_in(own, 3), number_of)
    source_of, receiver = mixed[0:number_of // 2 * 2:2], mixed[1:number_of // 2 * 2:2]
    room = jnp.minimum(tallies[source_of] - 1, limit - tallies[receiver]) // 2
    room = jnp.where((source_of == order[0]) | (receiver == order[0]) | (tallies[receiver] == 0), 0, jnp.maximum(room, 0))
    shifted = jax.random.randint(jax.random.fold_in(own, 4), (number_of // 2,), 0, 1 << 20) % (room + 1)
    tallies = tallies.at[source_of].add(-shifted).at[receiver].add(shifted)
    labels = jnp.searchsorted(jnp.cumsum(tallies), jnp.arange(rows * top), side="right").astype(jnp.int32)
    listing = labels.reshape(top, rows).T
    listing = listing[jax.random.permutation(jax.random.fold_in(own, 1), rows)]
    rotation = jax.random.randint(jax.random.fold_in(own, 2), (rows, 1), 0, top)
    return jnp.take_along_axis(listing, (jnp.arange(top)[None, :] + rotation) % top, axis=1)


def portions_of(number_of, total, bound, slope, full):
    weights = [(1 << 20) // math.isqrt(grade ** slope) + 1 for grade in range(1, number_of + 1)]
    largest = bound if full else min(bound, max(-(-total // number_of), total * weights[0] // sum(weights)))
    least = 1 if total - largest >= number_of - 1 else 0
    counts, rest = [largest] + [least] * (number_of - 1), total - largest - least * (number_of - 1)
    while rest > 0:
        movable = [i for i in range(1, number_of) if counts[i] < largest] or [i for i in range(1, number_of) if counts[i] < bound]
        whole, budget = sum([weights[i] for i in movable]), rest
        for i in movable:
            addition = min(bound - counts[i], max(1, budget * weights[i] // whole), rest)
            counts[i] = counts[i] + addition
            rest = rest - addition
    return np.array(counts)


def normal_values(own_key, shape, width, most, pieces=(), kind=jnp.bfloat16):
    entries = width * jax.random.normal(own_key, shape, jnp.float32)
    if pieces:
        entries = entries * levels(own_key, shape, pieces, -0.22, 0.18)
    return jnp.clip(entries, -most, most).astype(kind)


def setup_inputs(seed: int = 0) -> dict:
    streams_of = jax.random.split(jax.random.key(seed), 8)
    tokens = normal_values(streams_of[0], (TOKENS, D), 1.0, 6.0, ((0, 256),))
    routes_keys = jax.random.split(jax.random.fold_in(streams_of[1], 1), TOKENS // TOK_DEV)
    routes_turns = jax.random.permutation(jax.random.fold_in(streams_of[1], 3), TOKENS // TOK_DEV)
    routes = jax.vmap(lambda own, number: assign_block(jax.random.fold_in(streams_of[1], 2), own, number, TOK_DEV, EXPERTS, 2, MOST, 2))(routes_keys, routes_turns).reshape((TOKENS, 2))
    gates = jnp.clip(0.2 + 0.8 * jax.random.uniform(streams_of[2], (TOKENS, 2), jnp.float32) ** levels(streams_of[2], (TOKENS, 2), ((0, 256),), -0.2, 0.2), 0.2, 1.0)
    out_grad = normal_values(streams_of[3], (TOKENS, D), 1.0, 6.0, ((0, 256),))
    gate_weight = normal_values(streams_of[4], (EXPERTS, D, FF), D ** -0.5, 0.09375, ((0, 4), (2, 64)))
    up_weight = normal_values(streams_of[5], (EXPERTS, D, FF), D ** -0.5, 0.09375, ((0, 4), (2, 64)))
    down_weight = normal_values(streams_of[6], (EXPERTS, FF, D), FF ** -0.5, 0.046875, ((0, 4), (1, 64)))
    return {"tokens": tokens, "routes": routes, "gates": gates, "out_grad": out_grad, "gate_weight": gate_weight, "up_weight": up_weight, "down_weight": down_weight}


def contract(left_side, right_side, left_dim, right_dim):
    return lax.dot_general(left_side, right_side, (((left_dim,), (right_dim,)), ((), ())), preferred_element_type=jnp.float32)


def expert_rows(rows_x, rows_dy, w_gate, w_up, w_down):
    gate_act = jnp.dot(rows_x, w_gate, preferred_element_type=jnp.float32)
    up_act = jnp.dot(rows_x, w_up, preferred_element_type=jnp.float32)
    sigmoid_gate = jax.nn.sigmoid(gate_act)
    silu_gate = gate_act * sigmoid_gate
    hidden = (silu_gate * up_act).astype(jnp.bfloat16)
    hidden_grad = contract(rows_dy, w_down, 1, 1)
    gate_grad = (hidden_grad * up_act * sigmoid_gate * (1.0 + gate_act * (1.0 - sigmoid_gate))).astype(jnp.bfloat16)
    up_grad = (hidden_grad * silu_gate).astype(jnp.bfloat16)
    return hidden, gate_grad, up_grad


def reference(tokens, routes, gates, out_grad, gate_weight, up_weight, down_weight):
    blocks = N_EXPERT * N_FSDP
    flat_routes = routes.reshape(blocks, TOK_DEV * 2).astype(jnp.int32)
    expert_ids = jnp.arange(EXPERTS, dtype=jnp.int32)
    onehot = (flat_routes[:, :, None] == expert_ids[None, None, :]).astype(jnp.int32)
    earlier = jnp.cumsum(onehot, axis=1) - onehot
    slot_of = jnp.sum(earlier * onehot, axis=2).astype(jnp.int32)
    block_ids = jnp.arange(blocks, dtype=jnp.int32)[:, None]
    target = ((flat_routes * blocks + block_ids) * MOST + slot_of).reshape(-1).astype(jnp.int32)
    token_pairs = jnp.repeat(tokens, 2, axis=0)
    contrib = (gates[:, :, None] * out_grad[:, None, :].astype(jnp.float32)).astype(jnp.bfloat16)
    contrib = contrib.reshape(TOKENS * 2, D)
    rows_total = EXPERTS * blocks * MOST
    rows_x = jnp.zeros((rows_total, D), jnp.bfloat16).at[target].set(token_pairs)
    rows_dy = jnp.zeros((rows_total, D), jnp.bfloat16).at[target].set(contrib)

    def per_expert(operands):
        expert_x, expert_dy, w_gate, w_up, w_down = operands
        hidden, gate_grad, up_grad = expert_rows(expert_x, expert_dy, w_gate, w_up, w_down)
        grad_gate = contract(expert_x, gate_grad, 0, 0).astype(jnp.bfloat16)
        grad_up = contract(expert_x, up_grad, 0, 0).astype(jnp.bfloat16)
        grad_down = contract(hidden, expert_dy, 0, 0).astype(jnp.bfloat16)
        row_grad = (contract(gate_grad, w_gate, 1, 1) + contract(up_grad, w_up, 1, 1)).astype(jnp.bfloat16)
        return grad_gate, grad_up, grad_down, row_grad

    results = lax.map(per_expert, (rows_x.reshape(EXPERTS, blocks * MOST, D), rows_dy.reshape(EXPERTS, blocks * MOST, D), gate_weight, up_weight, down_weight))
    row_grad = results[3].reshape(rows_total, D)
    pair_grad = jnp.take(row_grad, target, axis=0).astype(jnp.float32).reshape(TOKENS, 2, D)
    tokens_grad = jnp.sum(pair_grad, axis=1).astype(jnp.bfloat16)
    return tokens_grad, results[0], results[1], results[2]
```

```python
import functools

import jax
import jax.numpy as jnp
from jax import lax
from jax.experimental import pallas as pl
from jax.experimental.pallas import tpu as pltpu
from jax.sharding import PartitionSpec as P

MESH = pl.DeviceIdType.MESH
BF = jnp.bfloat16
F32 = jnp.float32
D = 4096
SL = 128
CB = 8 * SL
W = D + 128
CA = W - CB
HW = D // 2


def gather_kernel(p_ref, big, stk, zbuf, blk, s1, r1, sp, rp, sa, ra, sb, rb, sf, rf, szp, rzp, szm, rzm, ssib, rsib):
    e=lax.axis_index("expert"); f=lax.axis_index("fsdp")
    c=e%2; zl=e//2; zh=f%4; z=zh*2+zl; x=f//16; y=(f//4)%4
    c0=1-c
    i1=y*c0+x*c; i2=x*c0+y*c
    st1=4*c0+16*c; st2=16*c0+4*c
    def dv(a,b): return {"expert":e,"fsdp":(a%4)*st1+(b%4)*st2+zh}
    def bj(a,b): return ((a%4)*st1+(b%4)*st2)//4
    def dz(zz,cc): return {"expert":(zz%2)*2+cc,"fsdp":(f//4)*4+zz//2}
    def rc(src,dst,ss,rs,d):
        return pltpu.make_async_remote_copy(src_ref=src,dst_ref=dst,send_sem=ss,recv_sem=rs,device_id=d,device_id_type=MESH)
    bar=pltpu.get_barrier_semaphore()
    zoff=[(dd,cc) for dd in range(8) for cc in range(2) if (dd,cc)!=(0,0)]
    poff=[(a,b) for a in range(4) for b in range(4) if (a,b)!=(0,0)]
    for dd,cc in zoff: pl.semaphore_signal(bar,inc=1,device_id=dz((z+dd)%8,(c+cc)%2),device_id_type=MESH)
    for a,b in poff: pl.semaphore_signal(bar,inc=1,device_id=dv(i1+a,i2+b),device_id_type=MESH)
    stk[...]=p_ref[...]
    pl.semaphore_wait(bar,30)
    me=z*2+c
    c1=[]
    order=sorted(range(15),key=lambda i:-min(zoff[i][0],8-zoff[i][0]))
    for i in order:
        dd,cc=zoff[i]
        cp=rc(stk.at[(c+cc)%2],zbuf.at[me],s1.at[i],r1.at[i],dz((z+dd)%8,(c+cc)%2)); cp.start(); c1.append(cp)
    zbuf[me]=stk[c]
    for i in reversed(order):
        dd,cc=zoff[i]
        src=((z+8-dd)%8)*2+(c+cc)%2
        rc(stk.at[0],zbuf.at[src],s1.at[i],r1.at[i],dz(0,0)).wait_recv()
    for i in range(16):
        blk[2*i:2*i+2,:]=zbuf[i].astype(F32)
    jo=bj(i1,i2)
    big[c,jo,:,CB:W]=blk[:,CB:W].astype(BF)
    mycol=pl.ds(pl.multiple_of(SL*z,128),SL)
    big[c,jo,:,mycol]=blk[:,mycol].astype(BF)
    for cp in c1: cp.wait_send()
    sends=[]
    for i,(a,b) in enumerate(poff):
        cp=rc(big.at[c,jo,:,mycol],big.at[c,jo,:,mycol],sp.at[i],rp.at[i],dv(i1+a,i2+b)); cp.start(); sends.append(cp)
    A=lambda j: big.at[c,j,:,CB:W]
    def a2send(k,a):
        j=bj(i1+a,i2)
        for t,s in ((0,1),(1,-1)):
            cp=rc(A(j),A(j),sb.at[2*k+t],rb.at[2*k+t],dv(i1,i2+s)); cp.start(); sends.append(cp)
    for a in (1,3,2):
        cp=rc(A(jo),A(jo),sa.at[a-1],ra.at[a-1],dv(i1+a,i2)); cp.start(); sends.append(cp)
    a2send(0,0)
    sibn=[0]
    sib={"expert":zl*2+c0,"fsdp":f}
    sibw=[]
    def sibsend(ref, oref):
        i=sibn[0]; sibn[0]+=1
        cp=rc(ref,ref,ssib.at[i],rsib.at[i],sib); cp.start(); sends.append(cp)
        sibw.append((oref,i))
    o_i1=i2; o_i2=i1
    def obj(a,b): return ((a%4)*st2+(b%4)*st1)//4
    def AO(j): return big.at[c0,j,:,CB:W]
    sibsend(A(jo),AO(obj(o_i1,o_i2)))
    for i,(a,b) in enumerate(poff):
        j=bj(i1-a+4,i2-b+4)
        rc(big.at[c,jo,:,mycol],big.at[c,j,:,mycol],sp.at[i],rp.at[i],dv(0,0)).wait_recv()
    def zc(k): return pl.ds(pl.multiple_of(SL*((z+k+8)%8),128),SL)
    S=lambda k: big.at[c,:,:,zc(k)]
    SO=lambda k: big.at[c0,:,:,zc(k)]
    H=lambda k,h: big.at[c,8*h:8*h+8,:,zc(k)]
    def zsend(h):
        if h<3:
            cp=rc(S(-h),S(-h),szp.at[h],rzp.at[h],dz((z+1)%8,c)); cp.start(); sends.append(cp)
            cp=rc(S(h),S(h),szm.at[h],rzm.at[h],dz((z+7)%8,c)); cp.start(); sends.append(cp)
        else:
            cp=rc(H(-3,0),H(-3,0),szp.at[3],rzp.at[3],dz((z+1)%8,c)); cp.start(); sends.append(cp)
            cp=rc(H(3,1),H(3,1),szm.at[3],rzm.at[3],dz((z+7)%8,c)); cp.start(); sends.append(cp)
    def zrecv(h):
        if h<3:
            rc(S(0),S(-h-1),szp.at[h],rzp.at[h],dz(0,0)).wait_recv()
            rc(S(0),S(h+1),szm.at[h],rzm.at[h],dz(0,0)).wait_recv()
            sibsend(S(-h-1),SO(-h-1)); sibsend(S(h+1),SO(h+1))
        else:
            rc(H(0,0),H(-4,0),szp.at[3],rzp.at[3],dz(0,0)).wait_recv()
            rc(H(0,1),H(4,1),szm.at[3],rzm.at[3],dz(0,0)).wait_recv()
            sibsend(S(4),SO(4))
    zsend(0)
    sibsend(S(0),SO(0))
    for a in (1,3,2):
        j=bj(i1-a+4,i2)
        rc(A(jo),A(j),sa.at[a-1],ra.at[a-1],dv(0,0)).wait_recv()
        a2send(a,4-a)
        sibsend(A(j),AO(obj(o_i1-a+4,o_i2)))
    AH=lambda j,h: big.at[c,j,16*h:16*h+16,CB:W]
    def a2recv(k,a):
        jm=bj(i1+a,i2+3); jp=bj(i1+a,i2+1)
        rc(A(jo),A(jm),sb.at[2*k],rb.at[2*k],dv(0,0)).wait_recv()
        cp=rc(AH(jm,0),AH(jm,0),sf.at[2*k],rf.at[2*k],dv(i1,i2+1)); cp.start(); sends.append(cp)
        rc(A(jo),A(jp),sb.at[2*k+1],rb.at[2*k+1],dv(0,0)).wait_recv()
        cp=rc(AH(jp,1),AH(jp,1),sf.at[2*k+1],rf.at[2*k+1],dv(i1,i2+3)); cp.start(); sends.append(cp)
        sibsend(A(jm),AO(obj(o_i1+a,o_i2+3)))
        sibsend(A(jp),AO(obj(o_i1+a,o_i2+1)))
    def a2fin(k,a):
        j=bj(i1+a,i2+2)
        rc(AH(jo,0),AH(j,0),sf.at[2*k],rf.at[2*k],dv(0,0)).wait_recv()
        rc(AH(jo,1),AH(j,1),sf.at[2*k+1],rf.at[2*k+1],dv(0,0)).wait_recv()
        sibsend(A(j),AO(obj(o_i1+a,o_i2+2)))
    ks=[(0,0),(1,3),(3,1),(2,2)]
    zrecv(0); zsend(1)
    a2recv(*ks[0])
    zrecv(1); zsend(2)
    a2recv(*ks[1])
    a2recv(*ks[2])
    zrecv(2); zsend(3)
    a2fin(*ks[0])
    a2recv(*ks[3])
    a2fin(*ks[1]); a2fin(*ks[2])
    zrecv(3)
    a2fin(*ks[3])
    for oref,i in sibw:
        rc(oref,oref,ssib.at[i],rsib.at[i],sib).wait_recv()
    for cp in sends: cp.wait_send()

def gather(payload):
    dma=pltpu.SemaphoreType.DMA
    return pl.pallas_call(gather_kernel,
        out_shape=jax.ShapeDtypeStruct((2,16,32,W),BF),
        in_specs=[pl.BlockSpec(memory_space=pltpu.VMEM)],out_specs=pl.BlockSpec(memory_space=pltpu.VMEM),
        scratch_shapes=[pltpu.VMEM((2,2,W),BF),pltpu.VMEM((16,2,W),BF),pltpu.VMEM((32,W),F32),
          dma((15,)),dma((15,)),dma((15,)),dma((15,)),dma((3,)),dma((3,)),dma((8,)),dma((8,)),dma((8,)),dma((8,)),dma((4,)),dma((4,)),dma((4,)),dma((4,)),dma((24,)),dma((24,))],
        compiler_params=pltpu.CompilerParams(collective_id=0,has_side_effects=True,vmem_limit_bytes=60<<20),name="gatherk")(payload)


def rs_kernel(pg, out, sbuf, acc0, r1, acc1, r2, acc2, zs, r3, ss0, rs0, ss1, rs1, ss2, rs2, ss3, rs3):
    e=lax.axis_index("expert"); f=lax.axis_index("fsdp")
    c=e%2; zl=e//2; zh=f%4; z=zh*2+zl; x=f//16; y=(f//4)%4
    c0=1-c
    i1=y*c0+x*c; i2=x*c0+y*c
    st1=4*c0+16*c; st2=16*c0+4*c
    def dv(a,b): return {"expert":e,"fsdp":(a%4)*st1+(b%4)*st2+zh}
    def bj(a,b): return ((a%4)*st1+(b%4)*st2)//4
    def dz(zz,cc): return {"expert":(zz%2)*2+cc,"fsdp":(f//4)*4+zz//2}
    def rc(src,dst,ss,rs,d):
        return pltpu.make_async_remote_copy(src_ref=src,dst_ref=dst,send_sem=ss,recv_sem=rs,device_id=d,device_id_type=MESH)
    bar=pltpu.get_barrier_semaphore()
    zoff=[(dd,cc) for dd in range(8) for cc in range(2) if (dd,cc)!=(0,0)]
    for dd,cc in zoff: pl.semaphore_signal(bar,inc=1,device_id=dz((z+dd)%8,(c+cc)%2),device_id_type=MESH)
    for a in (1,2,3):
        pl.semaphore_signal(bar,inc=1,device_id=dv(i1+a,i2),device_id_type=MESH)
        pl.semaphore_signal(bar,inc=1,device_id=dv(i1,i2+a),device_id_type=MESH)
    pl.semaphore_wait(bar,21)
    sib={"expert":zl*2+c0,"fsdp":f}
    mine=pl.ds(pl.multiple_of(c*HW,128),HW); other=pl.ds(pl.multiple_of(c0*HW,128),HW)
    sends=[]
    for j in range(16):
        cp=rc(pg.at[j,:,other],sbuf.at[j],ss0.at[j],rs0.at[j],sib); cp.start(); sends.append(cp)
    for j in range(16):
        rc(pg.at[j,:,other],sbuf.at[j],ss0.at[j],rs0.at[j],sib).wait_recv()
    def addj(j,_):
        acc0[j]=(pg[j,:,mine].astype(F32)+sbuf[j].astype(F32)).astype(BF)
        return 0
    for b in (2,1,3):
        for a in range(4):
            addj(bj(a,i2+b),0)
        for a in range(4):
            j=bj(a,i2+b)
            i=(b-1)*4+a
            cp=rc(acc0.at[j],r1.at[b-1,a],ss1.at[i],rs1.at[i],dv(i1,i2+b)); cp.start(); sends.append(cp)
    for b in (1,3,2):
        for a in range(4):
            i=(b-1)*4+a
            rc(acc0.at[0],r1.at[b-1,a],ss1.at[i],rs1.at[i],dv(0,0)).wait_recv()
    def sum1(a):
        j=bj(a,i2)
        ai=a%4
        return pg[j,:,mine].astype(F32)+sbuf[j].astype(F32)+r1[0,ai].astype(F32)+r1[1,ai].astype(F32)+r1[2,ai].astype(F32)
    for k,a in enumerate((2,1,3)):
        acc1[a-1]=sum1(i1+a).astype(BF)
        cp=rc(acc1.at[a-1],r2.at[a-1],ss2.at[a-1],rs2.at[a-1],dv(i1+a,i2)); cp.start(); sends.append(cp)
    acc2[...]=sum1(i1)
    for a in (1,3,2):
        rc(acc1.at[0],r2.at[a-1],ss2.at[a-1],rs2.at[a-1],dv(0,0)).wait_recv()
    acc2[...]=acc2[...]+r2[0].astype(F32)+r2[1].astype(F32)+r2[2].astype(F32)
    for i in range(16):
        zs[i]=acc2[2*i:2*i+2,:].astype(BF)
    order=sorted(range(15),key=lambda i:-min(zoff[i][0],8-zoff[i][0]))
    for i in order:
        dd,cc=zoff[i]
        t=((z+dd)%8)*2+(c+cc)%2
        cp=rc(zs.at[t],r3.at[z,c],ss3.at[i],rs3.at[i],dz((z+dd)%8,(c+cc)%2)); cp.start(); sends.append(cp)
    r3[z,c]=zs[z*2+c]
    for i in reversed(order):
        dd,cc=zoff[i]
        rc(zs.at[0],r3.at[(z+8-dd)%8,(c+cc)%2],ss3.at[i],rs3.at[i],dz(0,0)).wait_recv()
    for h in range(2):
        s=r3[0,h].astype(F32)
        for k in range(1,8): s=s+r3[k,h].astype(F32)
        out[:,h*HW:(h+1)*HW]=s.astype(BF)
    for cp in sends: cp.wait_send()

def rscat(pg,cid=1):
    dma=pltpu.SemaphoreType.DMA; V=pltpu.VMEM
    return pl.pallas_call(rs_kernel,
        out_shape=jax.ShapeDtypeStruct((2,4096),BF),
        in_specs=[pl.BlockSpec(memory_space=V)],out_specs=pl.BlockSpec(memory_space=V),
        scratch_shapes=[V((16,32,HW),BF),V((16,32,HW),BF),V((3,4,32,HW),BF),V((3,32,HW),BF),V((3,32,HW),BF),V((32,HW),F32),V((16,2,HW),BF),V((8,2,2,HW),BF),
          dma((16,)),dma((16,)),dma((12,)),dma((12,)),dma((3,)),dma((3,)),dma((15,)),dma((15,))],
        compiler_params=pltpu.CompilerParams(collective_id=cid,has_side_effects=True,vmem_limit_bytes=60<<20),name="rsk")(pg)


def contract(left, right, left_dim, right_dim):
    return lax.dot_general(left, right, (((left_dim,), (right_dim,)), ((), ())), preferred_element_type=F32)


def per_device(tokens, routes, gates, out_grad, gate_weight, up_weight, down_weight):
    expert_ids = jnp.arange(4, dtype=jnp.int32)
    dense = jnp.sum(jnp.where(routes[:, :, None] == expert_ids, gates[:, :, None], 0.0), axis=1)
    high = lax.reduce_precision(dense, 8, 7)
    middle = lax.reduce_precision(dense - high, 8, 7)
    low = dense - high - middle
    codes = jnp.concatenate([high, middle, low, jnp.zeros((2, 116), F32)], axis=1).astype(BF)
    payload = jnp.stack(
        [jnp.concatenate([tokens, codes], axis=1), jnp.concatenate([out_grad, codes], axis=1)]
    )
    big = gather(payload).reshape(2, 512, W)
    rows_x = big[0, :, :D]
    rows_dy = big[1, :, :D]
    e = lax.axis_index("expert")
    lane = jnp.arange(128, dtype=jnp.int32)
    own = (lane % 4 == e) & (lane < 12)
    gate = jnp.sum(jnp.where(own, big[1, :, D:].astype(F32), 0.0), axis=1, keepdims=True)
    w_gate = gate_weight[0]
    w_up = up_weight[0]
    w_down = down_weight[0]
    gate_act = contract(rows_x, w_gate, 1, 0)
    up_act = contract(rows_x, w_up, 1, 0)
    sigmoid_gate = jax.nn.sigmoid(gate_act)
    silu_gate = gate_act * sigmoid_gate
    hidden = (gate * (silu_gate * up_act)).astype(BF)
    hidden_grad = gate * contract(rows_dy, w_down, 1, 1)
    gate_grad = (hidden_grad * up_act * sigmoid_gate * (1.0 + gate_act * (1.0 - sigmoid_gate))).astype(BF)
    up_grad = (hidden_grad * silu_gate).astype(BF)
    partial = (contract(gate_grad, w_gate, 1, 1) + contract(up_grad, w_up, 1, 1)).astype(BF)
    tokens_grad = rscat(partial.reshape(16, 32, D))
    return (
        tokens_grad,
        contract(rows_x, gate_grad, 0, 0).astype(BF)[None],
        contract(rows_x, up_grad, 0, 0).astype(BF)[None],
        contract(hidden, rows_dy, 0, 0).astype(BF)[None],
    )


def solution(mesh):
    return jax.shard_map(
        per_device,
        mesh=mesh,
        in_specs=(
            P(("expert", "fsdp"), None),
            P(("expert", "fsdp"), None),
            P(("expert", "fsdp"), None),
            P(("expert", "fsdp"), None),
            P("expert", None, "fsdp"),
            P("expert", None, "fsdp"),
            P("expert", "fsdp", None),
        ),
        out_specs=(
            P(("expert", "fsdp"), None),
            P("expert", None, "fsdp"),
            P("expert", None, "fsdp"),
            P("expert", "fsdp", None),
        ),
        check_vma=False,
    )
```

```python
import jax
import jax.numpy as jnp
from jax import lax
from jax.experimental import pallas as pl
from jax.experimental.pallas import tpu as pltpu
from jax.sharding import PartitionSpec as P

MESH = pl.DeviceIdType.MESH
BF = jnp.bfloat16
F32 = jnp.float32
D = 4096
FB = 256
SL = 128
CB = 8 * SL
W = D + 128
HW = D // 2
QC = 512
NQ = HW // QC


def mm(left, right):
    return lax.dot_general(left, right, (((1,), (0,)), ((), ())), preferred_element_type=F32)


def mmt(left, right):
    return lax.dot_general(left, right, (((1,), (1,)), ((), ())), preferred_element_type=F32)


def main_kernel(
    tok_ref, route_ref, gate_ref, og_ref, wg_hbm, wu_hbm, wd_hbm,
    out, bigo, guo, hso,
    big, stk, zbuf, blk, wg, wu, wd, act_g, act_u, act_h, gu, hs,
    pgo, sbuf, acc, own1, r1, acc1, r2, own2, zs, r3,
    wsem, osem, s1, rv1, sp, rp, sa, ra, sb, rb, sf, rf, szp, rzp, szm, rzm, ssib, rsib,
    ss0, rs0, ss1, rs1, ss2, rs2, ss3, rs3,
):
    e = lax.axis_index("expert")
    f = lax.axis_index("fsdp")
    c = e % 2
    zl = e // 2
    zh = f % 4
    z = zh * 2 + zl
    x = f // 16
    y = (f // 4) % 4
    c0 = 1 - c
    i1 = y * c0 + x * c
    i2 = x * c0 + y * c
    st1 = 4 * c0 + 16 * c
    st2 = 16 * c0 + 4 * c

    def dv(a, b):
        return {"expert": e, "fsdp": (a % 4) * st1 + (b % 4) * st2 + zh}

    def bj(a, b):
        return ((a % 4) * st1 + (b % 4) * st2) // 4

    def obj(a, b):
        return ((a % 4) * st2 + (b % 4) * st1) // 4

    def dz(zz, cc):
        return {"expert": (zz % 2) * 2 + cc, "fsdp": (f // 4) * 4 + zz // 2}

    sib = {"expert": zl * 2 + c0, "fsdp": f}

    def rc(src, dst, ss, rs, d):
        return pltpu.make_async_remote_copy(
            src_ref=src, dst_ref=dst, send_sem=ss, recv_sem=rs, device_id=d, device_id_type=MESH
        )

    sends = []

    def go(*args):
        cp = rc(*args)
        cp.start()
        sends.append(cp)

    bar = pltpu.get_barrier_semaphore()
    zoff = [(dd, cc) for dd in range(8) for cc in range(2) if (dd, cc) != (0, 0)]
    poff = [(a, b) for a in range(4) for b in range(4) if (a, b) != (0, 0)]
    for dd, cc in zoff:
        pl.semaphore_signal(bar, inc=1, device_id=dz((z + dd) % 8, (c + cc) % 2), device_id_type=MESH)
    for a, b in poff:
        pl.semaphore_signal(bar, inc=1, device_id=dv(i1 + a, i2 + b), device_id_type=MESH)
    loads = [
        pltpu.make_async_copy(wg_hbm.at[0], wg, wsem.at[0]),
        pltpu.make_async_copy(wu_hbm.at[0], wu, wsem.at[1]),
        pltpu.make_async_copy(wd_hbm.at[0], wd, wsem.at[2]),
    ]
    for cp in loads:
        cp.start()
    stk[0, :, 0:D] = tok_ref[...]
    stk[1, :, 0:D] = og_ref[...]
    lane = lax.broadcasted_iota(jnp.int32, (2, 128), 1)
    dense = jnp.zeros((2, 128), F32)
    for k in range(2):
        dense = dense + jnp.where(lane % 4 == route_ref[:, k : k + 1], gate_ref[:, k : k + 1], 0.0)
    high = dense.astype(BF).astype(F32)
    middle = (dense - high).astype(BF).astype(F32)
    low = dense - high - middle
    codes = jnp.where(lane < 4, high, jnp.where(lane < 8, middle, jnp.where(lane < 12, low, 0.0)))
    stk[0, :, D:W] = codes.astype(BF)
    stk[1, :, D:W] = codes.astype(BF)
    pl.semaphore_wait(bar, 30)

    order = sorted(range(15), key=lambda i: -min(zoff[i][0], 8 - zoff[i][0]))
    me = z * 2 + c
    for i in order:
        dd, cc = zoff[i]
        go(stk.at[(c + cc) % 2], zbuf.at[me], s1.at[i], rv1.at[i], dz((z + dd) % 8, (c + cc) % 2))
    zbuf[me] = stk[c]
    for i in reversed(order):
        dd, cc = zoff[i]
        src = ((z + 8 - dd) % 8) * 2 + (c + cc) % 2
        rc(stk.at[0], zbuf.at[src], s1.at[i], rv1.at[i], dz(0, 0)).wait_recv()
    for i in range(16):
        blk[2 * i : 2 * i + 2, :] = zbuf[i].astype(F32)
    jo = bj(i1, i2)
    mycol = pl.ds(pl.multiple_of(SL * z, 128), SL)
    big[c, jo, :, mycol] = blk[:, mycol].astype(BF)
    big[c, jo, :, CB:W] = blk[:, CB:W].astype(BF)

    for i, (a, b) in enumerate(poff):
        go(big.at[c, jo, :, mycol], big.at[c, jo, :, mycol], sp.at[i], rp.at[i], dv(i1 + a, i2 + b))

    def part(j):
        return big.at[c, j, :, CB:W]

    def opart(j):
        return big.at[c0, j, :, CB:W]

    def a2send(k, a):
        j = bj(i1 + a, i2)
        for t, s in ((0, 1), (1, 3)):
            go(part(j), part(j), sb.at[2 * k + t], rb.at[2 * k + t], dv(i1, i2 + s))

    for a in (1, 3, 2):
        go(part(jo), part(jo), sa.at[a - 1], ra.at[a - 1], dv(i1 + a, i2))
    a2send(0, 0)
    arrivals = {}

    def sibsend(key, ref, oref):
        i = len(arrivals)
        go(ref, ref, ssib.at[i], rsib.at[i], sib)
        arrivals[key] = (oref, i)

    def sibwait(key):
        oref, i = arrivals[key]
        rc(oref, oref, ssib.at[i], rsib.at[i], sib).wait_recv()

    sibsend((0, 0), part(jo), opart(obj(i2, i1)))
    for i, (a, b) in enumerate(poff):
        j = bj(i1 - a + 4, i2 - b + 4)
        rc(big.at[c, jo, :, mycol], big.at[c, j, :, mycol], sp.at[i], rp.at[i], dv(0, 0)).wait_recv()

    def zc(k):
        return pl.ds(pl.multiple_of(SL * ((z + k + 8) % 8), 128), SL)

    def zs_(k):
        return big.at[c, :, :, zc(k)]

    def zh_(k, h):
        return big.at[c, 8 * h : 8 * h + 8, :, zc(k)]

    def zsend(h):
        if h < 3:
            go(zs_(-h), zs_(-h), szp.at[h], rzp.at[h], dz((z + 1) % 8, c))
            go(zs_(h), zs_(h), szm.at[h], rzm.at[h], dz((z + 7) % 8, c))
        else:
            go(zh_(-3, 0), zh_(-3, 0), szp.at[3], rzp.at[3], dz((z + 1) % 8, c))
            go(zh_(3, 1), zh_(3, 1), szm.at[3], rzm.at[3], dz((z + 7) % 8, c))

    def zsib(k):
        sibsend(("z", k), zs_(k), big.at[c0, :, :, zc(k)])

    def zrecv(h):
        if h < 3:
            rc(zs_(0), zs_(-h - 1), szp.at[h], rzp.at[h], dz(0, 0)).wait_recv()
            rc(zs_(0), zs_(h + 1), szm.at[h], rzm.at[h], dz(0, 0)).wait_recv()
            zsib(-h - 1)
            zsib(h + 1)
        else:
            rc(zh_(0, 0), zh_(-4, 0), szp.at[3], rzp.at[3], dz(0, 0)).wait_recv()
            rc(zh_(0, 1), zh_(4, 1), szm.at[3], rzm.at[3], dz(0, 0)).wait_recv()
            zsib(4)

    zsend(0)
    zsib(0)
    for a in (1, 3, 2):
        j = bj(i1 - a + 4, i2)
        rc(part(jo), part(j), sa.at[a - 1], ra.at[a - 1], dv(0, 0)).wait_recv()
        a2send(a, 4 - a)
        sibsend((4 - a, 0), part(j), opart(obj(i2 - a + 4, i1)))

    def half(j, h):
        return big.at[c, j, 16 * h : 16 * h + 16, CB:W]

    def a2recv(k, a):
        jm = bj(i1 + a, i2 + 3)
        jp = bj(i1 + a, i2 + 1)
        rc(part(jo), part(jm), sb.at[2 * k], rb.at[2 * k], dv(0, 0)).wait_recv()
        go(half(jm, 0), half(jm, 0), sf.at[2 * k], rf.at[2 * k], dv(i1, i2 + 1))
        rc(part(jo), part(jp), sb.at[2 * k + 1], rb.at[2 * k + 1], dv(0, 0)).wait_recv()
        go(half(jp, 1), half(jp, 1), sf.at[2 * k + 1], rf.at[2 * k + 1], dv(i1, i2 + 3))
        sibsend((a, 3), part(jm), opart(obj(i2 + a, i1 + 3)))
        sibsend((a, 1), part(jp), opart(obj(i2 + a, i1 + 1)))

    def a2fin(k, a):
        j = bj(i1 + a, i2 + 2)
        rc(half(jo, 0), half(j, 0), sf.at[2 * k], rf.at[2 * k], dv(0, 0)).wait_recv()
        rc(half(jo, 1), half(j, 1), sf.at[2 * k + 1], rf.at[2 * k + 1], dv(0, 0)).wait_recv()
        sibsend((a, 2), part(j), opart(obj(i2 + a, i1 + 2)))

    def rows_of(arr, a):
        if arr == 0:
            return [t * 4 + (y + a) % 4 for t in range(4)]
        return [((x + a) % 4) * 4 + t for t in range(4)]

    def acts_a(offsets):
        for arr in (0, 1):
            js = [j for a in offsets for j in rows_of(arr, a)]
            left = jnp.concatenate([big[arr, j, :, CB:D] for j in js], axis=0)
            if arr == 0:
                made = ((act_g, mm(left, wg[CB:D, :])), (act_u, mm(left, wu[CB:D, :])))
            else:
                made = ((act_h, mmt(left, wd[:, CB:D])),)
            for ref, val in made:
                for i, j in enumerate(js):
                    ref[j] = val[32 * i : 32 * i + 32]

    zrecv(0)
    zsend(1)
    a2recv(0, 0)
    zrecv(1)
    zsend(2)
    a2recv(1, 3)
    a2recv(3, 1)
    zrecv(2)
    zsend(3)
    a2fin(0, 0)
    a2recv(2, 2)
    a2fin(1, 3)
    for cp in loads:
        cp.wait()
    for a in (0, 3):
        for b in range(4):
            sibwait((a, b))
    acts_a((0, 3))
    a2fin(3, 1)
    zrecv(3)
    a2fin(2, 2)
    for a in (1, 2):
        for b in range(4):
            sibwait((a, b))
    acts_a((1, 2))
    for k in range(-3, 5):
        sibwait(("z", k))
    save = [pltpu.make_async_copy(big, bigo, osem.at[0])]
    save[0].start()

    lane32 = lax.broadcasted_iota(jnp.int32, (128, 128), 1)
    own_lane = (lane32 % 4 == e) & (lane32 < 12)

    def hidden_rows(r, _):
        def get(arr, lo, hi):
            return big[arr, pl.ds(4 * r, 4), :, lo:hi].reshape(128, hi - lo)

        rows_x = get(0, 0, CB)
        g = act_g[pl.ds(4 * r, 4)].reshape(128, FB) + mm(rows_x, wg[0:CB, :])
        u = act_u[pl.ds(4 * r, 4)].reshape(128, FB) + mm(rows_x, wu[0:CB, :])
        h = act_h[pl.ds(4 * r, 4)].reshape(128, FB) + mmt(get(1, 0, CB), wd[:, 0:CB])
        gate = jnp.sum(jnp.where(own_lane, get(1, D, W).astype(F32), 0.0), axis=1, keepdims=True)
        sig = jax.nn.sigmoid(g)
        silu = g * sig
        h = h * gate
        hs[pl.ds(4 * r, 4)] = (gate * (silu * u)).astype(BF).reshape(4, 32, FB)
        gu[pl.ds(4 * r, 4), :, 0:FB] = (h * u * sig * (1.0 + g * (1.0 - sig))).astype(BF).reshape(4, 32, FB)
        gu[pl.ds(4 * r, 4), :, FB : 2 * FB] = (h * silu).astype(BF).reshape(4, 32, FB)
        return 0

    lax.fori_loop(0, 4, hidden_rows, 0)
    save += [
        pltpu.make_async_copy(gu, guo, osem.at[1]),
        pltpu.make_async_copy(hs, hso, osem.at[2]),
    ]
    save[1].start()
    save[2].start()

    js = [bj(i1 + a, i2 + b) for b in range(4) for a in range(4)]

    def share(q, half_of):
        cols = pl.ds(pl.multiple_of(half_of * HW + q * QC, QC), QC)
        left = jnp.concatenate([gu[j] for j in js], axis=0)
        return mmt(left[:, 0:FB], wg[cols, :]) + mmt(left[:, FB : 2 * FB], wu[cols, :])

    for q in range(NQ):
        pgo[q] = share(q, c0).astype(BF).reshape(16, 32, QC)
        go(pgo.at[q], sbuf.at[q], ss0.at[q], rs0.at[q], sib)
    for q in range(NQ):
        val = share(q, c).reshape(16, 32, QC)
        rc(pgo.at[q], sbuf.at[q], ss0.at[q], rs0.at[q], sib).wait_recv()
        for b in (2, 1, 3, 0):
            for a in range(4):
                s = val[b * 4 + a] + sbuf[q, a * 4 + b].astype(F32)
                if b:
                    acc[q, b - 1, a] = s.astype(BF)
                else:
                    own1[q, a] = s
            if b:
                i = q * 3 + b - 1
                go(acc.at[q, b - 1], r1.at[q, b - 1], ss1.at[i], rs1.at[i], dv(i1, i2 + b))
    for q in range(NQ):
        for b in (1, 3, 2):
            i = q * 3 + b - 1
            rc(acc.at[q, b - 1], r1.at[q, b - 1], ss1.at[i], rs1.at[i], dv(0, 0)).wait_recv()
        for a in (2, 1, 3, 0):
            s = own1[q, a] + r1[q, 0, a].astype(F32) + r1[q, 1, a].astype(F32) + r1[q, 2, a].astype(F32)
            if a:
                i = q * 3 + a - 1
                acc1[q, a - 1] = s.astype(BF)
                go(acc1.at[q, a - 1], r2.at[q, a - 1], ss2.at[i], rs2.at[i], dv(i1 + a, i2))
            else:
                own2[q] = s
    for q in range(NQ):
        for a in (1, 3, 2):
            i = q * 3 + a - 1
            rc(acc1.at[q, a - 1], r2.at[q, a - 1], ss2.at[i], rs2.at[i], dv(0, 0)).wait_recv()
        own2[q] = own2[q] + r2[q, 0].astype(F32) + r2[q, 1].astype(F32) + r2[q, 2].astype(F32)
        for i in range(16):
            zs[i, :, q * QC : q * QC + QC] = own2[q, 2 * i : 2 * i + 2, :].astype(BF)
    for i in order:
        dd, cc = zoff[i]
        to = ((z + dd) % 8) * 2 + (c + cc) % 2
        go(zs.at[to], r3.at[z, c], ss3.at[i], rs3.at[i], dz((z + dd) % 8, (c + cc) % 2))
    r3[z, c] = zs[me]
    for i in reversed(order):
        dd, cc = zoff[i]
        rc(zs.at[0], r3.at[(z + 8 - dd) % 8, (c + cc) % 2], ss3.at[i], rs3.at[i], dz(0, 0)).wait_recv()
    for h in range(2):
        s = r3[0, h].astype(F32)
        for k in range(1, 8):
            s = s + r3[k, h].astype(F32)
        out[:, h * HW : (h + 1) * HW] = s.astype(BF)
    for cp in sends:
        cp.wait_send()
    for cp in save:
        cp.wait()


def main_call(*args):
    dma = pltpu.SemaphoreType.DMA
    V = pltpu.VMEM
    vm = pl.BlockSpec(memory_space=V)
    hbm = pl.BlockSpec(memory_space=pl.ANY)
    return pl.pallas_call(
        main_kernel,
        out_shape=(
            jax.ShapeDtypeStruct((2, D), BF),
            jax.ShapeDtypeStruct((2, 16, 32, W), BF),
            jax.ShapeDtypeStruct((16, 32, 2 * FB), BF),
            jax.ShapeDtypeStruct((16, 32, FB), BF),
        ),
        in_specs=[vm, vm, vm, vm, hbm, hbm, hbm],
        out_specs=(vm, hbm, hbm, hbm),
        scratch_shapes=[
            V((2, 16, 32, W), BF), V((2, 2, W), BF), V((16, 2, W), BF), V((32, W), F32),
            V((D, FB), BF), V((D, FB), BF), V((FB, D), BF),
            V((16, 32, FB), F32), V((16, 32, FB), F32), V((16, 32, FB), F32),
            V((16, 32, 2 * FB), BF), V((16, 32, FB), BF),
            V((NQ, 16, 32, QC), BF), V((NQ, 16, 32, QC), BF), V((NQ, 3, 4, 32, QC), BF), V((NQ, 4, 32, QC), F32),
            V((NQ, 3, 4, 32, QC), BF), V((NQ, 3, 32, QC), BF), V((NQ, 3, 32, QC), BF), V((NQ, 32, QC), F32),
            V((16, 2, HW), BF), V((8, 2, 2, HW), BF),
            dma((3,)), dma((3,)), dma((15,)), dma((15,)), dma((15,)), dma((15,)), dma((3,)), dma((3,)),
            dma((8,)), dma((8,)), dma((8,)), dma((8,)), dma((4,)), dma((4,)), dma((4,)), dma((4,)),
            dma((24,)), dma((24,)), dma((NQ,)), dma((NQ,)), dma((3 * NQ,)), dma((3 * NQ,)),
            dma((3 * NQ,)), dma((3 * NQ,)), dma((15,)), dma((15,)),
        ],
        compiler_params=pltpu.CompilerParams(
            collective_id=0, has_side_effects=True, vmem_limit_bytes=60 << 20
        ),
        name="gather_compute_sum",
    )(*args)


def contract_rows(left, right):
    return lax.dot_general(left, right, (((0,), (0,)), ((), ())), preferred_element_type=F32)


def per_device(tokens, routes, gates, out_grad, gate_weight, up_weight, down_weight):
    tokens_grad, big, gu, hs = main_call(tokens, routes, gates, out_grad, gate_weight, up_weight, down_weight)
    big = big.reshape(2, 512, W)
    gu = gu.reshape(512, 2 * FB)
    return (
        tokens_grad,
        contract_rows(big[0, :, :D], gu[:, :FB]).astype(BF)[None],
        contract_rows(big[0, :, :D], gu[:, FB:]).astype(BF)[None],
        contract_rows(hs.reshape(512, FB), big[1, :, :D]).astype(BF)[None],
    )


def solution(mesh):
    return jax.shard_map(
        per_device,
        mesh=mesh,
        in_specs=(
            P(("expert", "fsdp"), None),
            P(("expert", "fsdp"), None),
            P(("expert", "fsdp"), None),
            P(("expert", "fsdp"), None),
            P("expert", None, "fsdp"),
            P("expert", None, "fsdp"),
            P("expert", "fsdp", None),
        ),
        out_specs=(
            P(("expert", "fsdp"), None),
            P("expert", None, "fsdp"),
            P("expert", None, "fsdp"),
            P("expert", "fsdp", None),
        ),
        check_vma=False,
    )
```

```python
import jax
import jax.numpy as jnp
from jax import lax
from jax.experimental import pallas as pl
from jax.experimental.pallas import tpu as pltpu
from jax.sharding import PartitionSpec as P

MESH = pl.DeviceIdType.MESH
BF = jnp.bfloat16
F32 = jnp.float32
D = 4096
FB = 256
SL = 128
CB = 8 * SL
W = D + 128
CM = (CB + D) // 2
SEG = ((CB, CM), (CM, W))
DATA = ((CB, CM), (CM, D))
SUB = 4
HW = D // 2
QC = 512
NQ = HW // QC


def mm(left, right):
    return lax.dot_general(left, right, (((1,), (0,)), ((), ())), preferred_element_type=F32)


def mmt(left, right):
    return lax.dot_general(left, right, (((1,), (1,)), ((), ())), preferred_element_type=F32)


def main_kernel(
    tok_ref, route_ref, gate_ref, og_ref, wg_hbm, wu_hbm, wd_hbm,
    out, dwg_hbm, dwu_hbm, dwd_hbm,
    big, stk, zbuf, blk, wg, wu, wd, act, gu, hs, hst, dwg, dwu, dwd,
    pgo, sbuf, far, far_in, near, kept, joined, own1, r1, acc1, r2, own2, zs, r3,
    wsem, osem, s1, rv1, sp, rp, sa, ra, sb, rb, sf, rf, szp, rzp, szm, rzm, ssib, rsib,
    ss0, rs0, ss1, rs1, ss2, rs2, ss3, rs3,
):
    e = lax.axis_index("expert")
    f = lax.axis_index("fsdp")
    c = lax.rem(e, 2)
    zl = lax.div(e, 2)
    xy = lax.div(f, 4)
    zh = lax.rem(f, 4)
    z = zh * 2 + zl
    x = lax.div(f, 16)
    y = lax.rem(xy, 4)
    c0 = 1 - c
    i1 = y * c0 + x * c
    i2 = x * c0 + y * c
    w1 = [lax.rem(i1 + a, 4) * (c0 + 4 * c) for a in range(4)]
    w2 = [lax.rem(i2 + a, 4) * (4 * c0 + c) for a in range(4)]
    zz = [lax.rem(z + d, 8) for d in range(8)]
    zdev = [(lax.rem(v, 2) * 2, xy * 4 + lax.div(v, 2)) for v in zz]
    core = [c, c0]

    def bj(a, b):
        return w1[a % 4] + w2[b % 4]

    def dv(a, b):
        return {"expert": e, "fsdp": bj(a, b) * 4 + zh}

    def dz(d, cc):
        return {"expert": zdev[d % 8][0] + core[cc], "fsdp": zdev[d % 8][1]}

    sib = {"expert": zl * 2 + c0, "fsdp": f}

    def rc(src, dst, ss, rs, d):
        return pltpu.make_async_remote_copy(
            src_ref=src, dst_ref=dst, send_sem=ss, recv_sem=rs, device_id=d, device_id_type=MESH
        )

    sends = []

    def go(*args):
        cp = rc(*args)
        cp.start()
        sends.append(cp)

    bar = pltpu.get_barrier_semaphore()
    zoff = [(dd, cc) for dd in range(8) for cc in range(2) if (dd, cc) != (0, 0)]
    poff = [(a, b) for a in range(4) for b in range(4) if (a, b) != (0, 0)]
    for dd, cc in zoff:
        pl.semaphore_signal(bar, inc=1, device_id=dz(dd, cc), device_id_type=MESH)
    for a, b in poff:
        pl.semaphore_signal(bar, inc=1, device_id=dv(a, b), device_id_type=MESH)
    loads = [
        pltpu.make_async_copy(wg_hbm.at[0], wg, wsem.at[0]),
        pltpu.make_async_copy(wu_hbm.at[0], wu, wsem.at[1]),
        pltpu.make_async_copy(wd_hbm.at[0], wd, wsem.at[2]),
    ]
    for cp in loads:
        cp.start()
    stk[0, :, 0:D] = tok_ref[...]
    stk[1, :, 0:D] = og_ref[...]
    lane = lax.broadcasted_iota(jnp.int32, (2, 128), 1)
    dense = jnp.zeros((2, 128), F32)
    for k in range(2):
        dense = dense + jnp.where(lane % 4 == route_ref[:, k : k + 1], gate_ref[:, k : k + 1], 0.0)
    high = dense.astype(BF).astype(F32)
    middle = (dense - high).astype(BF).astype(F32)
    low = dense - high - middle
    codes = jnp.where(lane < 4, high, jnp.where(lane < 8, middle, jnp.where(lane < 12, low, 0.0)))
    stk[0, :, D:W] = codes.astype(BF)
    stk[1, :, D:W] = codes.astype(BF)
    pl.semaphore_wait(bar, 30)

    order = sorted(range(15), key=lambda i: -min(zoff[i][0], 8 - zoff[i][0]))
    me = z * 2 + c
    line = ((0, CM), (CM, W))
    for t, (lo, hi) in enumerate(line):
        for i in order:
            dd, cc = zoff[i]
            go(
                stk.at[core[cc], :, lo:hi], zbuf.at[me, :, lo:hi], s1.at[15 * t + i], rv1.at[15 * t + i], dz(dd, cc)
            )
    zbuf[me] = stk[c]
    jo = bj(0, 0)
    mycol = pl.ds(pl.multiple_of(SL * z, 128), SL)

    def take_line(t):
        lo, hi = line[t]
        for i in reversed(order):
            dd, cc = zoff[i]
            src = zz[(8 - dd) % 8] * 2 + core[cc]
            rc(stk.at[0, :, lo:hi], zbuf.at[src, :, lo:hi], s1.at[15 * t + i], rv1.at[15 * t + i], sib).wait_recv()
        for i in range(16):
            blk[2 * i : 2 * i + 2, lo:hi] = zbuf[i, :, lo:hi].astype(F32)
        if t == 0:
            big[c, jo, :, mycol] = blk[:, mycol].astype(BF)
        lo, hi = SEG[t]
        big[c, jo, :, lo:hi] = blk[:, lo:hi].astype(BF)

    def gj(g, a, b):
        return bj(a, b) if g == 0 else bj(b, a)

    def gdv(g, a, b):
        return dv(a, b) if g == 0 else dv(b, a)

    def part(g, j):
        return big.at[c, j, :, SEG[g][0] : SEG[g][1]]

    def a2send(g, k, a):
        j = gj(g, a, 0)
        for t, s in ((0, 1), (1, 3)):
            i = 8 * g + 2 * k + t
            go(part(g, j), part(g, j), sb.at[i], rb.at[i], gdv(g, 0, s))

    arrivals = {}

    def sibsend(key, ref, oref=None):
        i = len(arrivals)
        go(ref, ref, ssib.at[i], rsib.at[i], sib)
        if oref is None:
            g, a, b = key
            oref = big.at[c0, gj(g, b, a), :, SEG[g][0] : SEG[g][1]]
        arrivals[key] = (oref, i)

    def sibwait(key):
        oref, i = arrivals[key]
        rc(oref, oref, ssib.at[i], rsib.at[i], sib).wait_recv()

    def own_send(g):
        for a in (1, 3, 2):
            i = 3 * g + a - 1
            go(part(g, jo), part(g, jo), sa.at[i], ra.at[i], gdv(g, a, 0))
        a2send(g, 0, 0)
        sibsend((g, 0, 0), part(g, jo))

    def a1recv(g):
        for a in (1, 3, 2):
            j = gj(g, 4 - a, 0)
            i = 3 * g + a - 1
            rc(part(g, jo), part(g, j), sa.at[i], ra.at[i], sib).wait_recv()
            a2send(g, a, 4 - a)
            sibsend((g, 4 - a, 0), part(g, j))

    def half(g, j, h):
        return big.at[c, j, 16 * h : 16 * h + 16, SEG[g][0] : SEG[g][1]]

    slot = {0: 0, 3: 1, 2: 2, 1: 3}

    def a2recv(g, a):
        for h, b in ((0, 3), (1, 1)):
            j = gj(g, a, b)
            i = 8 * g + 2 * slot[a] + h
            rc(part(g, jo), part(g, j), sb.at[i], rb.at[i], sib).wait_recv()
            go(half(g, j, h), half(g, j, h), sf.at[i], rf.at[i], gdv(g, 0, 4 - b))
        for b in (3, 1):
            sibsend((g, a, b), part(g, gj(g, a, b)))

    def a2fin(g, a):
        j = gj(g, a, 2)
        for h in range(2):
            i = 8 * g + 2 * slot[a] + h
            rc(half(g, jo, h), half(g, j, h), sf.at[i], rf.at[i], sib).wait_recv()
        sibsend((g, a, 2), part(g, j))

    def zc(k):
        return pl.ds(pl.multiple_of(SL * zz[k % 8], 128), SL)

    def piece(k, u):
        n = 16 // SUB
        return big.at[c, n * u : n * u + n, :, zc(k)]

    def zsend(h, u):
        i = SUB * h + u
        if h < 3 or u < SUB // 2:
            go(piece(-h, u), piece(-h, u), szp.at[i], rzp.at[i], dz(1, 0))
        if h < 3 or u >= SUB // 2:
            go(piece(h, u), piece(h, u), szm.at[i], rzm.at[i], dz(7, 0))

    def zsib(k):
        sibsend(("z", k), big.at[c, :, :, zc(k)], big.at[c0, :, :, zc(k)])

    def zrecv(h):
        for u in range(SUB):
            i = SUB * h + u
            if h < 3 or u < SUB // 2:
                rc(piece(0, u), piece(-h - 1, u), szp.at[i], rzp.at[i], sib).wait_recv()
            if h < 3 or u >= SUB // 2:
                rc(piece(0, u), piece(h + 1, u), szm.at[i], rzm.at[i], sib).wait_recv()
            if h < 3:
                zsend(h + 1, u)
        zsib(-h - 1)
        if h < 3:
            zsib(h + 1)

    take_line(0)
    for i, (a, b) in enumerate(poff):
        go(big.at[c, jo, :, mycol], big.at[c, jo, :, mycol], sp.at[i], rp.at[i], dv(a, b))
    own_send(0)
    take_line(1)
    own_send(1)
    for i, (a, b) in enumerate(poff):
        rc(big.at[c, jo, :, mycol], big.at[c, bj(4 - a, 4 - b), :, mycol], sp.at[i], rp.at[i], sib).wait_recv()
    for u in range(SUB):
        zsend(0, u)
    zsib(0)

    def rows_of(arr, a):
        if arr == 0:
            return [t * 4 + lax.rem(y + a, 4) for t in range(4)]
        return [lax.rem(x + a, 4) * 4 + t for t in range(4)]

    def acts(t, arr, js, lo, hi):
        left = jnp.concatenate([big[arr, j, :, lo:hi] for j in js], axis=0)
        if arr == 0:
            made = ((0, mm(left, wg[lo:hi, :])), (1, mm(left, wu[lo:hi, :])))
        else:
            made = ((2, mmt(left, wd[:, lo:hi])),)
        for n, val in made:
            for i, j in enumerate(js):
                act[t, n, j] = val[32 * i : 32 * i + 32]

    def acts_a(g, offsets):
        for a in offsets:
            for b in range(4):
                sibwait((g, a, b))
        for arr in (0, 1):
            acts(g, arr, [j for a in offsets for j in rows_of(arr ^ g, a)], *DATA[g])

    a1recv(0)
    a2recv(0, 0)
    zrecv(0)
    a1recv(1)
    a2recv(0, 3)
    zrecv(1)
    a2recv(1, 0)
    a2recv(0, 1)
    a2fin(0, 0)
    zrecv(2)
    a2recv(0, 2)
    a2recv(1, 3)
    a2recv(1, 1)
    a2fin(0, 3)
    a2fin(0, 1)
    a2fin(1, 0)
    a2recv(1, 2)
    for cp in loads:
        cp.wait()
    acts_a(0, (0, 3))
    zrecv(3)
    a2fin(0, 2)
    a2fin(1, 3)
    a2fin(1, 1)
    acts_a(0, (1, 2))
    a2fin(1, 2)
    acts_a(1, (0, 3))
    for k in range(-4, 4):
        sibwait(("z", k))
    for arr in (0, 1):
        acts(2, arr, list(range(16)), 0, CB)
    acts_a(1, (1, 2))

    lane32 = lax.broadcasted_iota(jnp.int32, (128, 128), 1)
    own_lane = (lane32 % 4 == e) & (lane32 < 12)

    def hidden_rows(r, _):
        def get(arr, lo, hi):
            return big[arr, pl.ds(4 * r, 4), :, lo:hi].reshape(128, hi - lo)

        def added(n):
            return sum(act[t, n, pl.ds(4 * r, 4)].reshape(128, FB) for t in range(3))

        g = added(0)
        u = added(1)
        h = added(2)
        gate = jnp.sum(jnp.where(own_lane, get(1, D, W).astype(F32), 0.0), axis=1, keepdims=True)
        sig = jax.nn.sigmoid(g)
        silu = g * sig
        h = h * gate
        hs[pl.ds(4 * r, 4)] = (gate * (silu * u)).astype(BF).reshape(4, 32, FB)
        gu[pl.ds(4 * r, 4), :, 0:FB] = (h * u * sig * (1.0 + g * (1.0 - sig))).astype(BF).reshape(4, 32, FB)
        gu[pl.ds(4 * r, 4), :, FB : 2 * FB] = (h * silu).astype(BF).reshape(4, 32, FB)
        return 0

    lax.fori_loop(0, 4, hidden_rows, 0)
    save = []

    def store(refs):
        for a, b in refs:
            cp = pltpu.make_async_copy(a, b, osem.at[len(save)])
            cp.start()
            save.append(cp)

    def weight_grads(t):
        cols = slice(512 * t, 512 * t + 512)
        val = lax.dot_general(
            big[0, :, :, cols].reshape(512, 512),
            gu[...].reshape(512, 2 * FB),
            (((0,), (0,)), ((), ())),
            preferred_element_type=F32,
        ).astype(BF)
        dwg[cols, :] = val[:, 0:FB]
        dwu[cols, :] = val[:, FB : 2 * FB]
        dwd[:, cols] = mm(hst[...], big[1, :, :, cols].reshape(512, 512)).astype(BF)
        store(
            [
                (dwg.at[cols, :], dwg_hbm.at[0, cols, :]),
                (dwu.at[cols, :], dwu_hbm.at[0, cols, :]),
                (dwd.at[:, cols], dwd_hbm.at[0, :, cols]),
            ]
        )

    def sj(q, a, b):
        return bj(a, b) if q % 2 == 0 else bj(b, a)

    def sdv(q, a, b):
        return dv(a, b) if q % 2 == 0 else dv(b, a)

    def share(q, half_of):
        cols = pl.ds(pl.multiple_of(half_of * HW + q * QC, QC), QC)
        left = jnp.concatenate([gu[sj(q, a, b)] for b in range(4) for a in range(4)], axis=0)
        return mmt(left[:, 0:FB], wg[cols, :]) + mmt(left[:, FB : 2 * FB], wu[cols, :])

    def sum_send(q):
        val = share(q, c).reshape(16, 32, QC)
        rc(pgo.at[q], sbuf.at[q], ss0.at[q], rs0.at[q], sib).wait_recv()

        def at(a, b):
            return val[b * 4 + a] + sbuf[q, a * 4 + b].astype(F32)

        for a in range(4):
            far[q, a] = at(a, 2).astype(BF)
        for h, b in ((0, 1), (1, 3)):
            i = 6 * q + h
            go(far.at[q, 2 * h : 2 * h + 2], far_in.at[q, h], ss1.at[i], rs1.at[i], sdv(q, 0, b))
        for h, b in ((0, 1), (1, 3)):
            i = 6 * q + 2 + h
            for a in range(2):
                near[q, h, a] = at(2 - 2 * h + a, b).astype(BF)
                kept[q, h, a] = at(2 * h + a, b)
            go(near.at[q, h], r1.at[q, h, 2 - 2 * h : 4 - 2 * h], ss1.at[i], rs1.at[i], sdv(q, 0, b))
        for a in range(4):
            own1[q, a] = at(a, 0)

    def join(q):
        for h, b in ((0, 1), (1, 3)):
            i = 6 * q + h
            rc(far.at[q, 0:2], far_in.at[q, h], ss1.at[i], rs1.at[i], sib).wait_recv()
            joined[q, h] = (kept[q, h] + far_in[q, h].astype(F32)).astype(BF)
            i = 6 * q + 4 + h
            go(joined.at[q, h], r1.at[q, h, 2 * h : 2 * h + 2], ss1.at[i], rs1.at[i], sdv(q, 0, b))

    def second(q):
        for h in range(2):
            for i, lo in ((6 * q + 2 + h, 2 - 2 * h), (6 * q + 4 + h, 2 * h)):
                rc(near.at[q, h], r1.at[q, h, lo : lo + 2], ss1.at[i], rs1.at[i], sib).wait_recv()
        for a in (2, 1, 3, 0):
            s = own1[q, a] + r1[q, 0, a].astype(F32) + r1[q, 1, a].astype(F32)
            if a:
                i = q * 3 + a - 1
                acc1[q, a - 1] = s.astype(BF)
                go(acc1.at[q, a - 1], r2.at[q, a - 1], ss2.at[i], rs2.at[i], sdv(q, a, 0))
            else:
                own2[q] = s

    def third(q):
        for a in (1, 3, 2):
            i = q * 3 + a - 1
            rc(acc1.at[q, a - 1], r2.at[q, a - 1], ss2.at[i], rs2.at[i], sib).wait_recv()
        own2[q] = own2[q] + r2[q, 0].astype(F32) + r2[q, 1].astype(F32) + r2[q, 2].astype(F32)
        for i in range(16):
            zs[q // 2, i, :, q % 2 * QC : q % 2 * QC + QC] = own2[q, 2 * i : 2 * i + 2, :].astype(BF)

    def line_send(t):
        for i in order:
            dd, cc = zoff[i]
            go(zs.at[t, zz[dd] * 2 + core[cc]], r3.at[t, z, c], ss3.at[15 * t + i], rs3.at[15 * t + i], dz(dd, cc))
        r3[t, z, c] = zs[t, me]

    def line_sum(t):
        for i in reversed(order):
            dd, cc = zoff[i]
            here = r3.at[t, zz[(8 - dd) % 8], core[cc]]
            rc(zs.at[t, 0], here, ss3.at[15 * t + i], rs3.at[15 * t + i], sib).wait_recv()
        for h in range(2):
            s = r3[t, 0, h].astype(F32)
            for k in range(1, 8):
                s = s + r3[t, k, h].astype(F32)
            out[:, h * HW + t * HW // 2 : h * HW + (t + 1) * HW // 2] = s.astype(BF)

    for q in range(NQ):
        pgo[q] = share(q, c0).astype(BF).reshape(16, 32, QC)
        go(pgo.at[q], sbuf.at[q], ss0.at[q], rs0.at[q], sib)
    for q in range(NQ):
        sum_send(q)
        if q:
            join(q - 1)
    hst[...] = hs[...].reshape(512, FB).astype(F32).T.astype(BF)
    join(NQ - 1)
    weight_grads(0)
    second(0)
    weight_grads(1)
    second(1)
    weight_grads(2)
    second(2)
    weight_grads(3)
    second(3)
    third(0)
    third(1)
    line_send(0)
    weight_grads(4)
    third(2)
    third(3)
    line_send(1)
    weight_grads(5)
    weight_grads(6)
    weight_grads(7)
    line_sum(0)
    line_sum(1)
    for cp in sends:
        cp.wait_send()
    for cp in save:
        cp.wait()


def main_call(*args):
    dma = pltpu.SemaphoreType.DMA
    V = pltpu.VMEM
    vm = pl.BlockSpec(memory_space=V)
    hbm = pl.BlockSpec(memory_space=pl.ANY)
    return pl.pallas_call(
        main_kernel,
        out_shape=(
            jax.ShapeDtypeStruct((2, D), BF),
            jax.ShapeDtypeStruct((1, D, FB), BF),
            jax.ShapeDtypeStruct((1, D, FB), BF),
            jax.ShapeDtypeStruct((1, FB, D), BF),
        ),
        in_specs=[vm, vm, vm, vm, hbm, hbm, hbm],
        out_specs=(vm, hbm, hbm, hbm),
        scratch_shapes=[
            V((2, 16, 32, W), BF), V((2, 2, W), BF), V((16, 2, W), BF), V((32, W), F32),
            V((D, FB), BF), V((D, FB), BF), V((FB, D), BF),
            V((3, 3, 16, 32, FB), F32),
            V((16, 32, 2 * FB), BF), V((16, 32, FB), BF), V((FB, 512), BF),
            V((D, FB), BF), V((D, FB), BF), V((FB, D), BF),
            V((NQ, 16, 32, QC), BF), V((NQ, 16, 32, QC), BF), V((NQ, 4, 32, QC), BF), V((NQ, 2, 2, 32, QC), BF),
            V((NQ, 2, 2, 32, QC), BF), V((NQ, 2, 2, 32, QC), F32), V((NQ, 2, 2, 32, QC), BF), V((NQ, 4, 32, QC), F32),
            V((NQ, 2, 4, 32, QC), BF), V((NQ, 3, 32, QC), BF), V((NQ, 3, 32, QC), BF), V((NQ, 32, QC), F32),
            V((2, 16, 2, HW // 2), BF), V((2, 8, 2, 2, HW // 2), BF),
            dma((3,)), dma((24,)), dma((30,)), dma((30,)), dma((15,)), dma((15,)), dma((6,)), dma((6,)),
            dma((16,)), dma((16,)), dma((16,)), dma((16,)), dma((4 * SUB,)), dma((4 * SUB,)), dma((4 * SUB,)), dma((4 * SUB,)),
            dma((40,)), dma((40,)), dma((NQ,)), dma((NQ,)), dma((6 * NQ,)), dma((6 * NQ,)),
            dma((3 * NQ,)), dma((3 * NQ,)), dma((30,)), dma((30,)),
        ],
        compiler_params=pltpu.CompilerParams(
            collective_id=0, has_side_effects=True, vmem_limit_bytes=60 << 20
        ),
        name="gather_compute_sum",
    )(*args)


def copy_kernel(*refs):
    loads, stores = [], []
    for a, b, held in zip(refs[0:4], refs[4:8], refs[8:12]):
        pieces = 4 if a.shape[0] == 1 else 1
        n = a.shape[1] // pieces
        for i in range(pieces):
            at = (slice(None), slice(n * i, n * i + n)) if pieces > 1 else (slice(None), slice(None))
            loads.append(pltpu.make_async_copy(a.at[at], held.at[at], refs[12].at[len(loads)]))
            stores.append(pltpu.make_async_copy(held.at[at], b.at[at], refs[13].at[len(stores)]))
    for cp in loads:
        cp.start()
    for load, cp in zip(loads, stores):
        load.wait()
        cp.start()
    for cp in stores:
        cp.wait()


def per_device(tokens, routes, gates, out_grad, gate_weight, up_weight, down_weight):
    results = main_call(tokens, routes, gates, out_grad, gate_weight, up_weight, down_weight)
    hbm = pl.BlockSpec(memory_space=pl.ANY)
    return pl.pallas_call(
        copy_kernel,
        out_shape=tuple(jax.ShapeDtypeStruct(a.shape, a.dtype) for a in results),
        in_specs=[hbm] * 4,
        out_specs=(hbm,) * 4,
        scratch_shapes=[pltpu.VMEM(a.shape, a.dtype) for a in results] + [pltpu.SemaphoreType.DMA((13,))] * 2,
        name="copy_results",
    )(*results)


def solution(mesh):
    return jax.shard_map(
        per_device,
        mesh=mesh,
        in_specs=(
            P(("expert", "fsdp"), None),
            P(("expert", "fsdp"), None),
            P(("expert", "fsdp"), None),
            P(("expert", "fsdp"), None),
            P("expert", None, "fsdp"),
            P("expert", None, "fsdp"),
            P("expert", "fsdp", None),
        ),
        out_specs=(
            P(("expert", "fsdp"), None),
            P("expert", None, "fsdp"),
            P("expert", None, "fsdp"),
            P("expert", "fsdp", None),
        ),
        check_vma=False,
    )
```

```python
import jax
import jax.numpy as jnp
from jax import lax
from jax.experimental import pallas as pl
from jax.experimental.pallas import tpu as pltpu
from jax.sharding import PartitionSpec as P

MESH = pl.DeviceIdType.MESH
BF = jnp.bfloat16
F32 = jnp.float32
D = 4096
FB = 256
SL = 128
CB = 8 * SL
W = D + 128
CM = (CB + D) // 2
SEG = ((CB, CM), (CM, W))
DATA = ((CB, CM), (CM, D))
SUB = 4
HW = D // 2
QC = 512
NQ = HW // QC


def mm(left, right):
    return lax.dot_general(left, right, (((1,), (0,)), ((), ())), preferred_element_type=F32)


def mmt(left, right):
    return lax.dot_general(left, right, (((1,), (1,)), ((), ())), preferred_element_type=F32)


def main_kernel(
    tok_hbm, route_hbm, gate_hbm, og_hbm, wg_hbm, wu_hbm, wd_hbm,
    out, dwg_hbm, dwu_hbm, dwd_hbm,
    route_ref, gate_ref, big, stk, zbuf, blk, wg, wu, wd, act, gu, hs, hst, dwg, dwu, dwd,
    pgo, sbuf, far, far_in, last_in, last_near, near, kept, joined, own1, r1, acc1, r2, own2, zs, r3,
    isem, wsem, osem, s1, rv1, sp, rp, sa, ra, rb, rf, sz, rzp, rzm, ssib, rsib,
    ss0, rs0, ss1, rs1, ss2, rs2, ss3, rs3,
):
    e = lax.axis_index("expert")
    f = lax.axis_index("fsdp")
    c = lax.rem(e, 2)
    zl = lax.div(e, 2)
    xy = lax.div(f, 4)
    zh = lax.rem(f, 4)
    z = zh * 2 + zl
    x = lax.div(f, 16)
    y = lax.rem(xy, 4)
    c0 = 1 - c
    i1 = y * c0 + x * c
    i2 = x * c0 + y * c
    w1 = [lax.rem(i1 + a, 4) * (c0 + 4 * c) for a in range(4)]
    w2 = [lax.rem(i2 + a, 4) * (4 * c0 + c) for a in range(4)]
    zz = [lax.rem(z + d, 8) for d in range(8)]
    zdev = [(lax.rem(v, 2) * 2, xy * 4 + lax.div(v, 2)) for v in zz]
    core = [c, c0]

    def bj(a, b):
        return w1[a % 4] + w2[b % 4]

    def dv(a, b):
        return {"expert": e, "fsdp": bj(a, b) * 4 + zh}

    def dz(d, cc):
        return {"expert": zdev[d % 8][0] + core[cc], "fsdp": zdev[d % 8][1]}

    sib = {"expert": zl * 2 + c0, "fsdp": f}

    def rc(src, dst, ss, rs, d):
        return pltpu.make_async_remote_copy(
            src_ref=src, dst_ref=dst, send_sem=ss, recv_sem=rs, device_id=d, device_id_type=MESH
        )

    def go(*args):
        rc(*args).start()

    def sent(ref, sem):
        rc(ref, ref, sem, sem, sib).wait_send()

    def came(ref, sem):
        rc(ref, ref, sem, sem, sib).wait_recv()

    inputs = [
        pltpu.make_async_copy(route_hbm, route_ref, isem.at[0]),
        pltpu.make_async_copy(gate_hbm, gate_ref, isem.at[1]),
        pltpu.make_async_copy(tok_hbm, stk.at[0, :, 0:D], isem.at[2]),
        pltpu.make_async_copy(og_hbm, stk.at[1, :, 0:D], isem.at[3]),
    ]
    for cp in inputs:
        cp.start()
    bar = pltpu.get_barrier_semaphore()
    zoff = [(dd, cc) for dd in range(8) for cc in range(2) if (dd, cc) != (0, 0)]
    poff = [(a, b) for a in range(4) for b in range(4) if (a, b) != (0, 0)]
    for dd, cc in zoff:
        pl.semaphore_signal(bar, inc=1, device_id=dz(dd, cc), device_id_type=MESH)
    for a, b in poff:
        pl.semaphore_signal(bar, inc=1, device_id=dv(a, b), device_id_type=MESH)
    loads = [
        pltpu.make_async_copy(wg_hbm.at[0], wg, wsem.at[0]),
        pltpu.make_async_copy(wu_hbm.at[0], wu, wsem.at[1]),
        pltpu.make_async_copy(wd_hbm.at[0], wd, wsem.at[2]),
    ]
    for cp in loads:
        cp.start()
    for cp in inputs:
        cp.wait()
    lane = lax.broadcasted_iota(jnp.int32, (2, 128), 1)
    dense = jnp.zeros((2, 128), F32)
    for k in range(2):
        dense = dense + jnp.where(lane % 4 == route_ref[:, k : k + 1], gate_ref[:, k : k + 1], 0.0)
    high = dense.astype(BF).astype(F32)
    middle = (dense - high).astype(BF).astype(F32)
    low = dense - high - middle
    codes = jnp.where(lane < 4, high, jnp.where(lane < 8, middle, jnp.where(lane < 12, low, 0.0)))
    stk[0, :, D:W] = codes.astype(BF)
    stk[1, :, D:W] = codes.astype(BF)
    pl.semaphore_wait(bar, 30)

    order = sorted(range(15), key=lambda i: -min(zoff[i][0], 8 - zoff[i][0]))
    me = z * 2 + c
    line = ((0, CM), (CM, W))
    for t, (lo, hi) in enumerate(line):
        for i in order:
            dd, cc = zoff[i]
            go(
                stk.at[core[cc], :, lo:hi], zbuf.at[me, :, lo:hi], s1.at[t], rv1.at[t], dz(dd, cc)
            )
    zbuf[me] = stk[c]
    jo = bj(0, 0)
    mycol = pl.ds(pl.multiple_of(SL * z, 128), SL)

    def take_line(t):
        lo, hi = line[t]
        came(zbuf.at[0:15, :, lo:hi], rv1.at[t])
        for i in range(16):
            blk[2 * i : 2 * i + 2, lo:hi] = zbuf[i, :, lo:hi].astype(F32)
        if t == 0:
            big[c, jo, :, mycol] = blk[:, mycol].astype(BF)
        lo, hi = SEG[t]
        big[c, jo, :, lo:hi] = blk[:, lo:hi].astype(BF)

    def gj(g, a, b):
        return bj(a, b) if g == 0 else bj(b, a)

    def gdv(g, a, b):
        return dv(a, b) if g == 0 else dv(b, a)

    def part(g, j):
        return big.at[c, j, :, SEG[g][0] : SEG[g][1]]

    def a2send(g, k, a):
        j = gj(g, a, 0)
        for t, s in ((0, 1), (1, 3)):
            i = 8 * g + 2 * k + t
            go(part(g, j), part(g, j), sa.at[g], rb.at[i], gdv(g, 0, s))

    def group(g, a):
        return 2 * g + (1 if a in (1, 2) else 0)

    def sibsend(g, a, ref):
        go(ref, ref, ssib, rsib.at[group(g, a)], sib)

    def own_send(g):
        for a in (1, 3, 2):
            i = 3 * g + a - 1
            go(part(g, jo), part(g, jo), sa.at[g], ra.at[i], gdv(g, a, 0))
        a2send(g, 0, 0)
        sibsend(g, 0, part(g, jo))

    def a1recv(g):
        for a in (1, 3, 2):
            j = gj(g, 4 - a, 0)
            i = 3 * g + a - 1
            came(part(g, j), ra.at[i])
            a2send(g, a, 4 - a)
            sibsend(g, 4 - a, part(g, j))

    def half(g, j, h):
        return big.at[c, j, 16 * h : 16 * h + 16, SEG[g][0] : SEG[g][1]]

    slot = {0: 0, 3: 1, 2: 2, 1: 3}

    def a2recv(g, a):
        for h, b in ((0, 3), (1, 1)):
            j = gj(g, a, b)
            i = 8 * g + 2 * slot[a] + h
            came(part(g, j), rb.at[i])
            go(half(g, j, h), half(g, j, h), sa.at[g], rf.at[4 * g + slot[a]], gdv(g, 0, 4 - b))
        for b in (3, 1):
            sibsend(g, a, part(g, gj(g, a, b)))

    def a2fin(g, a):
        j = gj(g, a, 2)
        came(part(g, j), rf.at[4 * g + slot[a]])
        sibsend(g, a, part(g, j))

    def zc(k):
        return pl.ds(pl.multiple_of(SL * zz[k % 8], 128), SL)

    def piece(k, u):
        n = 16 // SUB
        return big.at[c, n * u : n * u + n, :, zc(k)]

    def zsend(h, u):
        i = SUB * h + u
        if h < 3 or u < SUB // 2:
            go(piece(-h, u), piece(-h, u), sz, rzp.at[i], dz(1, 0))
        if h < 3 or u >= SUB // 2:
            go(piece(h, u), piece(h, u), sz, rzm.at[i], dz(7, 0))

    def zsib(k):
        go(big.at[c, :, :, zc(k)], big.at[c, :, :, zc(k)], ssib, rsib.at[4], sib)

    def zrecv(h):
        for u in range(SUB):
            i = SUB * h + u
            if h < 3 or u < SUB // 2:
                came(piece(-h - 1, u), rzp.at[i])
            if h < 3 or u >= SUB // 2:
                came(piece(h + 1, u), rzm.at[i])
            if h < 3:
                zsend(h + 1, u)
        zsib(-h - 1)
        if h < 3:
            zsib(h + 1)

    take_line(0)
    for a, b in poff:
        go(big.at[c, jo, :, mycol], big.at[c, jo, :, mycol], sp, rp, dv(a, b))
    own_send(0)
    take_line(1)
    own_send(1)
    came(big.at[c, 0:15, :, mycol], rp)
    for u in range(SUB):
        zsend(0, u)
    zsib(0)

    def rows_of(arr, a):
        if arr == 0:
            return [t * 4 + lax.rem(y + a, 4) for t in range(4)]
        return [lax.rem(x + a, 4) * 4 + t for t in range(4)]

    def acts(t, arr, js, lo, hi):
        left = jnp.concatenate([big[arr, j, :, lo:hi] for j in js], axis=0)
        if arr == 0:
            made = ((0, mm(left, wg[lo:hi, :])), (1, mm(left, wu[lo:hi, :])))
        else:
            made = ((2, mmt(left, wd[:, lo:hi])),)
        for n, val in made:
            for i, j in enumerate(js):
                act[t, n, j] = val[32 * i : 32 * i + 32]

    def acts_a(g, offsets):
        came(big.at[c0, 0:8, :, SEG[g][0] : SEG[g][1]], rsib.at[group(g, offsets[0])])
        for arr in (0, 1):
            acts(g, arr, [j for a in offsets for j in rows_of(arr ^ g, a)], *DATA[g])

    a1recv(0)
    a2recv(0, 0)
    zrecv(0)
    a1recv(1)
    a2recv(0, 3)
    zrecv(1)
    a2recv(1, 0)
    a2recv(0, 1)
    a2fin(0, 0)
    zrecv(2)
    a2recv(0, 2)
    a2recv(1, 3)
    a2recv(1, 1)
    a2fin(0, 3)
    a2fin(0, 1)
    a2fin(1, 0)
    a2recv(1, 2)
    for cp in loads:
        cp.wait()
    acts_a(0, (0, 3))
    zrecv(3)
    a2fin(0, 2)
    a2fin(1, 3)
    a2fin(1, 1)
    acts_a(0, (1, 2))
    a2fin(1, 2)
    acts_a(1, (0, 3))
    came(big.at[c0, :, :, 0:CB], rsib.at[4])
    for arr in (0, 1):
        acts(2, arr, list(range(16)), 0, CB)
    acts_a(1, (1, 2))

    lane32 = lax.broadcasted_iota(jnp.int32, (128, 128), 1)
    own_lane = (lane32 % 4 == e) & (lane32 < 12)

    def hidden_rows(r, _):
        def get(arr, lo, hi):
            return big[arr, pl.ds(4 * r, 4), :, lo:hi].reshape(128, hi - lo)

        def added(n):
            return sum(act[t, n, pl.ds(4 * r, 4)].reshape(128, FB) for t in range(3))

        g = added(0)
        u = added(1)
        h = added(2)
        gate = jnp.sum(jnp.where(own_lane, get(1, D, W).astype(F32), 0.0), axis=1, keepdims=True)
        sig = jax.nn.sigmoid(g)
        silu = g * sig
        h = h * gate
        hs[pl.ds(4 * r, 4)] = (gate * (silu * u)).astype(BF).reshape(4, 32, FB)
        gu[pl.ds(4 * r, 4), :, 0:FB] = (h * u * sig * (1.0 + g * (1.0 - sig))).astype(BF).reshape(4, 32, FB)
        gu[pl.ds(4 * r, 4), :, FB : 2 * FB] = (h * silu).astype(BF).reshape(4, 32, FB)
        return 0

    lax.fori_loop(0, 4, hidden_rows, 0)
    def store(refs):
        for n, (a, b) in enumerate(refs):
            pltpu.make_async_copy(a, b, osem.at[n]).start()

    def weight_grads(t):
        cols = slice(512 * t, 512 * t + 512)
        val = lax.dot_general(
            big[0, :, :, cols].reshape(512, 512),
            gu[...].reshape(512, 2 * FB),
            (((0,), (0,)), ((), ())),
            preferred_element_type=F32,
        ).astype(BF)
        dwg[cols, :] = val[:, 0:FB]
        dwu[cols, :] = val[:, FB : 2 * FB]
        dwd[:, cols] = mm(hst[...], big[1, :, :, cols].reshape(512, 512)).astype(BF)
        store(
            [
                (dwg.at[cols, :], dwg_hbm.at[0, cols, :]),
                (dwu.at[cols, :], dwu_hbm.at[0, cols, :]),
                (dwd.at[:, cols], dwd_hbm.at[0, :, cols]),
            ]
        )

    def sj(q, a, b):
        return bj(a, b) if q % 2 == 0 else bj(b, a)

    def sdv(q, a, b):
        return dv(a, b) if q % 2 == 0 else dv(b, a)

    def share(q, half_of):
        cols = pl.ds(pl.multiple_of(half_of * HW + q * QC, QC), QC)
        left = jnp.concatenate([gu[sj(q, a, b)] for b in range(4) for a in range(4)], axis=0)
        return mmt(left[:, 0:FB], wg[cols, :]) + mmt(left[:, FB : 2 * FB], wu[cols, :])

    def sum_send(q):
        val = share(q, c).reshape(16, 32, QC)
        rc(pgo.at[q], sbuf.at[q], ss0, rs0.at[q], sib).wait_recv()

        def at(a, b):
            return val[b * 4 + a] + sbuf[q, a * 4 + b].astype(F32)

        for a in range(4):
            far[q, a] = at(a, 2).astype(BF)
        if q == NQ - 1:
            go(far.at[q], last_in, ss1, rs1.at[2 * q], sdv(q, 0, 2))
            for h, b in ((0, 1), (1, 3)):
                for a in range(4):
                    last_near[h, a] = at(a, b).astype(BF)
                go(last_near.at[h], r1.at[q, h], ss1, rs1.at[2 * q + 1], sdv(q, 0, b))
            for a in range(4):
                own1[q, a] = at(a, 0)
            return
        for h, b in ((0, 1), (1, 3)):
            go(far.at[q, 2 * h : 2 * h + 2], far_in.at[q, h], ss1, rs1.at[2 * q], sdv(q, 0, b))
        for h, b in ((0, 1), (1, 3)):
            for a in range(2):
                near[q, h, a] = at(2 - 2 * h + a, b).astype(BF)
                kept[q, h, a] = at(2 * h + a, b)
            go(near.at[q, h], r1.at[q, h, 2 - 2 * h : 4 - 2 * h], ss1, rs1.at[2 * q + 1], sdv(q, 0, b))
        for a in range(4):
            own1[q, a] = at(a, 0)

    def join(q):
        came(far_in.at[q], rs1.at[2 * q])
        for h, b in ((0, 1), (1, 3)):
            joined[q, h] = (kept[q, h] + far_in[q, h].astype(F32)).astype(BF)
            go(joined.at[q, h], r1.at[q, h, 2 * h : 2 * h + 2], ss1, rs1.at[2 * q + 1], sdv(q, 0, b))

    def second(q):
        last = q == NQ - 1
        if last:
            came(last_in, rs1.at[2 * q])
        came(r1.at[q], rs1.at[2 * q + 1])
        for a in (2, 1, 3, 0):
            s = own1[q, a] + r1[q, 0, a].astype(F32) + r1[q, 1, a].astype(F32)
            if last:
                s = s + last_in[a].astype(F32)
            if a:
                acc1[q, a - 1] = s.astype(BF)
                go(acc1.at[q, a - 1], r2.at[q, a - 1], ss2, rs2.at[q], sdv(q, a, 0))
            else:
                own2[q] = s

    def third(q):
        came(r2.at[q], rs2.at[q])
        own2[q] = own2[q] + r2[q, 0].astype(F32) + r2[q, 1].astype(F32) + r2[q, 2].astype(F32)
        for i in range(16):
            zs[q // 2, i, :, q % 2 * QC : q % 2 * QC + QC] = own2[q, 2 * i : 2 * i + 2, :].astype(BF)

    def line_send(t):
        for i in order:
            dd, cc = zoff[i]
            go(zs.at[t, zz[dd] * 2 + core[cc]], r3.at[t, z, c], ss3.at[t], rs3.at[t], dz(dd, cc))
        r3[t, z, c] = zs[t, me]

    def line_sum(t):
        came(zs.at[t, 0:15], rs3.at[t])
        for h in range(2):
            s = r3[t, 0, h].astype(F32)
            for k in range(1, 8):
                s = s + r3[t, k, h].astype(F32)
            out[:, h * HW + t * HW // 2 : h * HW + (t + 1) * HW // 2] = s.astype(BF)

    def other_half(q):
        pgo[q] = share(q, c0).astype(BF).reshape(16, 32, QC)
        go(pgo.at[q], sbuf.at[q], ss0, rs0.at[q], sib)

    other_half(0)
    other_half(1)
    sum_send(0)
    other_half(2)
    sum_send(1)
    other_half(3)
    join(0)
    sum_send(2)
    join(1)
    sum_send(3)
    hst[...] = hs[...].reshape(512, FB).astype(F32).T.astype(BF)
    join(2)
    weight_grads(0)
    second(0)
    weight_grads(1)
    second(1)
    weight_grads(2)
    second(2)
    weight_grads(3)
    third(0)
    third(1)
    line_send(0)
    second(3)
    weight_grads(4)
    third(2)
    third(3)
    line_send(1)
    weight_grads(5)
    weight_grads(6)
    weight_grads(7)
    line_sum(0)
    line_sum(1)
    for t, (lo, hi) in enumerate(line):
        sent(zbuf.at[0:15, :, lo:hi], s1.at[t])
        sent(zs.at[t, 0:15], ss3.at[t])
    sent(big.at[c, 0:15, :, mycol], sp)
    for g, (lo, hi) in enumerate(SEG):
        sent(big.at[c, 0:15, :, lo:hi], sa.at[g])
    sent(big.at[c, :, :, 0 : 7 * SL], sz)
    sent(big.at[c], ssib)
    sent(pgo, ss0)
    sent(pgo.at[0:3], ss1)
    sent(pgo.at[0, 0:12], ss2)
    for n, (a, b) in enumerate(((dwg, dwg_hbm), (dwu, dwu_hbm), (dwd, dwd_hbm))):
        pltpu.make_async_copy(a, b.at[0], osem.at[n]).wait()


def main_call(*args):
    dma = pltpu.SemaphoreType.DMA
    V = pltpu.VMEM
    vm = pl.BlockSpec(memory_space=V)
    hbm = pl.BlockSpec(memory_space=pl.ANY)
    return pl.pallas_call(
        main_kernel,
        out_shape=(
            jax.ShapeDtypeStruct((2, D), BF),
            jax.ShapeDtypeStruct((1, D, FB), BF),
            jax.ShapeDtypeStruct((1, D, FB), BF),
            jax.ShapeDtypeStruct((1, FB, D), BF),
        ),
        in_specs=[hbm] * 7,
        out_specs=(vm, hbm, hbm, hbm),
        scratch_shapes=[
            V((2, 2), jnp.int32), V((2, 2), F32), V((2, 16, 32, W), BF), V((2, 2, W), BF), V((16, 2, W), BF), V((32, W), F32),
            V((D, FB), BF), V((D, FB), BF), V((FB, D), BF),
            V((3, 3, 16, 32, FB), F32),
            V((16, 32, 2 * FB), BF), V((16, 32, FB), BF), V((FB, 512), BF),
            V((D, FB), BF), V((D, FB), BF), V((FB, D), BF),
            V((NQ, 16, 32, QC), BF), V((NQ, 16, 32, QC), BF), V((NQ, 4, 32, QC), BF), V((NQ, 2, 2, 32, QC), BF), V((4, 32, QC), BF), V((2, 4, 32, QC), BF),
            V((NQ, 2, 2, 32, QC), BF), V((NQ, 2, 2, 32, QC), F32), V((NQ, 2, 2, 32, QC), BF), V((NQ, 4, 32, QC), F32),
            V((NQ, 2, 4, 32, QC), BF), V((NQ, 3, 32, QC), BF), V((NQ, 3, 32, QC), BF), V((NQ, 32, QC), F32),
            V((2, 16, 2, HW // 2), BF), V((2, 8, 2, 2, HW // 2), BF),
            dma((4,)), dma((3,)), dma((3,)), dma((2,)), dma((2,)), dma, dma, dma((2,)), dma((6,)), dma((16,)), dma((8,)),
            dma, dma((4 * SUB,)), dma((4 * SUB,)), dma, dma((5,)), dma, dma((NQ,)), dma, dma((2 * NQ,)),
            dma, dma((NQ,)), dma((2,)), dma((2,)),
        ],
        compiler_params=pltpu.CompilerParams(
            collective_id=0, has_side_effects=True, vmem_limit_bytes=60 << 20
        ),
        name="gather_compute_sum",
    )(*args)


def copy_kernel(*refs):
    loads, stores = [], []
    for a, b, held in zip(refs[0:4], refs[4:8], refs[8:12]):
        pieces = 4 if a.shape[0] == 1 else 1
        n = a.shape[1] // pieces
        for i in range(pieces):
            at = (slice(None), slice(n * i, n * i + n)) if pieces > 1 else (slice(None), slice(None))
            loads.append(pltpu.make_async_copy(a.at[at], held.at[at], refs[12].at[len(loads)]))
            stores.append(pltpu.make_async_copy(held.at[at], b.at[at], refs[13].at[len(stores)]))
    for cp in loads:
        cp.start()
    for load, cp in zip(loads, stores):
        load.wait()
        cp.start()
    for cp in stores:
        cp.wait()


def per_device(tokens, routes, gates, out_grad, gate_weight, up_weight, down_weight):
    results = main_call(tokens, routes, gates, out_grad, gate_weight, up_weight, down_weight)
    hbm = pl.BlockSpec(memory_space=pl.ANY)
    return pl.pallas_call(
        copy_kernel,
        out_shape=tuple(jax.ShapeDtypeStruct(a.shape, a.dtype) for a in results),
        in_specs=[hbm] * 4,
        out_specs=(hbm,) * 4,
        scratch_shapes=[pltpu.VMEM(a.shape, a.dtype) for a in results] + [pltpu.SemaphoreType.DMA((13,))] * 2,
        name="copy_results",
    )(*results)


def solution(mesh):
    return jax.shard_map(
        per_device,
        mesh=mesh,
        in_specs=(
            P(("expert", "fsdp"), None),
            P(("expert", "fsdp"), None),
            P(("expert", "fsdp"), None),
            P(("expert", "fsdp"), None),
            P("expert", None, "fsdp"),
            P("expert", None, "fsdp"),
            P("expert", "fsdp", None),
        ),
        out_specs=(
            P(("expert", "fsdp"), None),
            P("expert", None, "fsdp"),
            P("expert", None, "fsdp"),
            P("expert", "fsdp", None),
        ),
        check_vma=False,
    )
```

```python
import jax
import jax.numpy as jnp
from jax import lax
from jax.experimental import pallas as pl
from jax.experimental.pallas import tpu as pltpu
from jax.sharding import PartitionSpec as P

MESH = pl.DeviceIdType.MESH
BF = jnp.bfloat16
F32 = jnp.float32
D = 4096
FB = 256
SL = 128
CB = 8 * SL
W = D + 128
CM = (CB + D) // 2
SEG = ((CB, CM), (CM, W))
DATA = ((CB, CM), (CM, D))
SUB = 4
HW = D // 2
QC = 512
NQ = HW // QC


def mm(left, right):
    return lax.dot_general(left, right, (((1,), (0,)), ((), ())), preferred_element_type=F32)


def mmt(left, right):
    return lax.dot_general(left, right, (((1,), (1,)), ((), ())), preferred_element_type=F32)


def main_kernel(
    tok_hbm, route_hbm, gate_hbm, og_hbm, wg_hbm, wu_hbm, wd_hbm,
    out, dwg_hbm, dwu_hbm, dwd_hbm,
    route_ref, gate_ref, big, stk, zbuf, blk, wg, wu, wd, act, gu, hs, hst, dwg, dwu, dwd,
    pgo, sbuf, far, far_in, last_in, last_near, near, kept, joined, own1, r1, acc1, r2, own2, zs, r3,
    isem, wsem, osem, s1, rv1, sp, rp, sa, ra, rb, rf, sz, rzp, rzm, ssib, rsib,
    ss0, rs0, ss1, rs1, ss2, rs2, ss3, rs3,
):
    e = lax.axis_index("expert")
    f = lax.axis_index("fsdp")
    c = lax.rem(e, 2)
    zl = lax.div(e, 2)
    xy = lax.div(f, 4)
    zh = lax.rem(f, 4)
    z = zh * 2 + zl
    x = lax.div(f, 16)
    y = lax.rem(xy, 4)
    c0 = 1 - c
    i1 = y * c0 + x * c
    i2 = x * c0 + y * c
    w1 = [lax.rem(i1 + a, 4) * (c0 + 4 * c) for a in range(4)]
    w2 = [lax.rem(i2 + a, 4) * (4 * c0 + c) for a in range(4)]
    zz = [lax.rem(z + d, 8) for d in range(8)]
    zdev = [(lax.rem(v, 2) * 2, xy * 4 + lax.div(v, 2)) for v in zz]
    core = [c, c0]

    def bj(a, b):
        return w1[a % 4] + w2[b % 4]

    def dv(a, b):
        return {"expert": e, "fsdp": bj(a, b) * 4 + zh}

    def dz(d, cc):
        return {"expert": zdev[d % 8][0] + core[cc], "fsdp": zdev[d % 8][1]}

    sib = {"expert": zl * 2 + c0, "fsdp": f}

    def rc(src, dst, ss, rs, d):
        return pltpu.make_async_remote_copy(
            src_ref=src, dst_ref=dst, send_sem=ss, recv_sem=rs, device_id=d, device_id_type=MESH
        )

    def go(*args):
        rc(*args).start()

    def sent(ref, sem):
        rc(ref, ref, sem, sem, sib).wait_send()

    def came(ref, sem):
        rc(ref, ref, sem, sem, sib).wait_recv()

    inputs = [
        pltpu.make_async_copy(route_hbm, route_ref, isem.at[0]),
        pltpu.make_async_copy(gate_hbm, gate_ref, isem.at[1]),
        pltpu.make_async_copy(tok_hbm, stk.at[0, :, 0:D], isem.at[2]),
        pltpu.make_async_copy(og_hbm, stk.at[1, :, 0:D], isem.at[3]),
    ]
    for cp in inputs:
        cp.start()
    bar = pltpu.get_barrier_semaphore()
    zoff = [(dd, cc) for dd in range(8) for cc in range(2) if (dd, cc) != (0, 0)]
    poff = [(a, b) for a in range(4) for b in range(4) if (a, b) != (0, 0)]
    for dd, cc in zoff:
        pl.semaphore_signal(bar, inc=1, device_id=dz(dd, cc), device_id_type=MESH)
    for a, b in poff:
        pl.semaphore_signal(bar, inc=1, device_id=dv(a, b), device_id_type=MESH)
    loads = [
        pltpu.make_async_copy(wg_hbm.at[0], wg, wsem.at[0]),
        pltpu.make_async_copy(wu_hbm.at[0], wu, wsem.at[1]),
        pltpu.make_async_copy(wd_hbm.at[0], wd, wsem.at[2]),
    ]
    for cp in loads:
        cp.start()
    for cp in inputs:
        cp.wait()
    lane = lax.broadcasted_iota(jnp.int32, (2, 128), 1)
    dense = jnp.zeros((2, 128), F32)
    for k in range(2):
        dense = dense + jnp.where(lane % 4 == route_ref[:, k : k + 1], gate_ref[:, k : k + 1], 0.0)
    high = dense.astype(BF).astype(F32)
    middle = (dense - high).astype(BF).astype(F32)
    low = dense - high - middle
    codes = jnp.where(lane < 4, high, jnp.where(lane < 8, middle, jnp.where(lane < 12, low, 0.0)))
    stk[0, :, D:W] = codes.astype(BF)
    stk[1, :, D:W] = codes.astype(BF)
    pl.semaphore_wait(bar, 30)

    order = sorted(range(15), key=lambda i: -min(zoff[i][0], 8 - zoff[i][0]))
    me = z * 2 + c
    line = ((0, CM), (CM, W))
    for t, (lo, hi) in enumerate(line):
        for i in order:
            dd, cc = zoff[i]
            go(
                stk.at[core[cc], :, lo:hi], zbuf.at[me, :, lo:hi], s1.at[t], rv1.at[t], dz(dd, cc)
            )
    zbuf[me] = stk[c]
    jo = bj(0, 0)
    mycol = pl.ds(pl.multiple_of(SL * z, 128), SL)

    def take_line(t):
        lo, hi = line[t]
        came(zbuf.at[0:15, :, lo:hi], rv1.at[t])
        for i in range(16):
            blk[2 * i : 2 * i + 2, lo:hi] = zbuf[i, :, lo:hi].astype(F32)
        if t == 0:
            big[c, jo, :, mycol] = blk[:, mycol].astype(BF)
        lo, hi = SEG[t]
        big[c, jo, :, lo:hi] = blk[:, lo:hi].astype(BF)

    def gj(g, a, b):
        return bj(a, b) if g == 0 else bj(b, a)

    def gdv(g, a, b):
        return dv(a, b) if g == 0 else dv(b, a)

    def part(g, j):
        return big.at[c, j, :, SEG[g][0] : SEG[g][1]]

    def a2send(g, k, a):
        j = gj(g, a, 0)
        for t, s in ((0, 1), (1, 3)):
            i = 8 * g + 2 * k + t
            go(part(g, j), part(g, j), sa.at[g], rb.at[i], gdv(g, 0, s))

    def group(g, a):
        return 2 * g + (1 if a in (1, 2) else 0)

    def sibsend(g, a, ref):
        go(ref, ref, ssib, rsib.at[group(g, a)], sib)

    def own_send(g):
        for a in (1, 3, 2):
            i = 3 * g + a - 1
            go(part(g, jo), part(g, jo), sa.at[g], ra.at[i], gdv(g, a, 0))
        a2send(g, 0, 0)
        sibsend(g, 0, part(g, jo))

    def a1recv(g):
        for a in (1, 3, 2):
            j = gj(g, 4 - a, 0)
            i = 3 * g + a - 1
            came(part(g, j), ra.at[i])
            a2send(g, a, 4 - a)
            sibsend(g, 4 - a, part(g, j))

    def half(g, j, h):
        return big.at[c, j, 16 * h : 16 * h + 16, SEG[g][0] : SEG[g][1]]

    slot = {0: 0, 3: 1, 2: 2, 1: 3}

    def a2recv(g, a):
        for h, b in ((0, 3), (1, 1)):
            j = gj(g, a, b)
            i = 8 * g + 2 * slot[a] + h
            came(part(g, j), rb.at[i])
            go(half(g, j, h), half(g, j, h), sa.at[g], rf.at[4 * g + slot[a]], gdv(g, 0, 4 - b))
        for b in (3, 1):
            sibsend(g, a, part(g, gj(g, a, b)))

    def a2fin(g, a):
        j = gj(g, a, 2)
        came(part(g, j), rf.at[4 * g + slot[a]])
        sibsend(g, a, part(g, j))

    def zc(k):
        return pl.ds(pl.multiple_of(SL * zz[k % 8], 128), SL)

    def piece(k, u):
        n = 16 // SUB
        return big.at[c, n * u : n * u + n, :, zc(k)]

    def zsend(h, u):
        i = SUB * h + u
        if h < 3 or u < SUB // 2:
            go(piece(-h, u), piece(-h, u), sz, rzp.at[i], dz(1, 0))
        if h < 3 or u >= SUB // 2:
            go(piece(h, u), piece(h, u), sz, rzm.at[i], dz(7, 0))

    def zsib(k):
        go(big.at[c, :, :, zc(k)], big.at[c, :, :, zc(k)], ssib, rsib.at[4], sib)

    def zrecv(h):
        for u in range(SUB):
            i = SUB * h + u
            if h < 3 or u < SUB // 2:
                came(piece(-h - 1, u), rzp.at[i])
            if h < 3 or u >= SUB // 2:
                came(piece(h + 1, u), rzm.at[i])
            if h < 3:
                zsend(h + 1, u)
        zsib(-h - 1)
        if h < 3:
            zsib(h + 1)

    take_line(0)
    for a, b in poff:
        go(big.at[c, jo, :, mycol], big.at[c, jo, :, mycol], sp, rp, dv(a, b))
    own_send(0)
    take_line(1)
    own_send(1)
    came(big.at[c, 0:15, :, mycol], rp)
    for u in range(SUB):
        zsend(0, u)
    zsib(0)

    def rows_of(arr, a):
        if arr == 0:
            return [t * 4 + lax.rem(y + a, 4) for t in range(4)]
        return [lax.rem(x + a, 4) * 4 + t for t in range(4)]

    def acts(t, arr, js, lo, hi):
        left = jnp.concatenate([big[arr, j, :, lo:hi] for j in js], axis=0)
        if arr == 0:
            made = ((0, mm(left, wg[lo:hi, :])), (1, mm(left, wu[lo:hi, :])))
        else:
            made = ((2, mmt(left, wd[:, lo:hi])),)
        for n, val in made:
            for i, j in enumerate(js):
                act[t, n, j] = val[32 * i : 32 * i + 32]

    def acts_a(g, offsets):
        came(big.at[c0, 0:8, :, SEG[g][0] : SEG[g][1]], rsib.at[group(g, offsets[0])])
        for arr in (0, 1):
            acts(g, arr, [j for a in offsets for j in rows_of(arr ^ g, a)], *DATA[g])

    a1recv(0)
    a2recv(0, 0)
    zrecv(0)
    a1recv(1)
    a2recv(0, 3)
    zrecv(1)
    a2recv(1, 0)
    a2recv(0, 1)
    a2fin(0, 0)
    zrecv(2)
    a2recv(0, 2)
    a2recv(1, 3)
    a2recv(1, 1)
    a2fin(0, 3)
    a2fin(0, 1)
    a2fin(1, 0)
    a2recv(1, 2)
    for cp in loads:
        cp.wait()
    acts_a(0, (0, 3))
    zrecv(3)
    a2fin(0, 2)
    a2fin(1, 3)
    a2fin(1, 1)
    acts_a(0, (1, 2))
    came(big.at[c0, :, :, 0:CB], rsib.at[4])
    for arr in (0, 1):
        acts(2, arr, list(range(16)), 0, CB)
    a2fin(1, 2)
    acts_a(1, (0, 3))
    acts_a(1, (1, 2))

    lane32 = lax.broadcasted_iota(jnp.int32, (128, 128), 1)
    own_lane = (lane32 % 4 == e) & (lane32 < 12)

    def hidden_rows(r, _):
        def get(arr, lo, hi):
            return big[arr, pl.ds(4 * r, 4), :, lo:hi].reshape(128, hi - lo)

        def added(n):
            return sum(act[t, n, pl.ds(4 * r, 4)].reshape(128, FB) for t in range(3))

        g = added(0)
        u = added(1)
        h = added(2)
        gate = jnp.sum(jnp.where(own_lane, get(1, D, W).astype(F32), 0.0), axis=1, keepdims=True)
        sig = jax.nn.sigmoid(g)
        silu = g * sig
        h = h * gate
        hs[pl.ds(4 * r, 4)] = (gate * (silu * u)).astype(BF).reshape(4, 32, FB)
        gu[pl.ds(4 * r, 4), :, 0:FB] = (h * u * sig * (1.0 + g * (1.0 - sig))).astype(BF).reshape(4, 32, FB)
        gu[pl.ds(4 * r, 4), :, FB : 2 * FB] = (h * silu).astype(BF).reshape(4, 32, FB)
        return 0

    lax.fori_loop(0, 4, hidden_rows, 0)
    def store(refs):
        for n, (a, b) in enumerate(refs):
            pltpu.make_async_copy(a, b, osem.at[n]).start()

    def weight_grads(t):
        cols = slice(512 * t, 512 * t + 512)
        val = lax.dot_general(
            big[0, :, :, cols].reshape(512, 512),
            gu[...].reshape(512, 2 * FB),
            (((0,), (0,)), ((), ())),
            preferred_element_type=F32,
        ).astype(BF)
        dwg[cols, :] = val[:, 0:FB]
        dwu[cols, :] = val[:, FB : 2 * FB]
        dwd[:, cols] = mm(hst[...], big[1, :, :, cols].reshape(512, 512)).astype(BF)
        store(
            [
                (dwg.at[cols, :], dwg_hbm.at[0, cols, :]),
                (dwu.at[cols, :], dwu_hbm.at[0, cols, :]),
                (dwd.at[:, cols], dwd_hbm.at[0, :, cols]),
            ]
        )

    def sj(q, a, b):
        return bj(a, b) if q % 2 == 0 else bj(b, a)

    def sdv(q, a, b):
        return dv(a, b) if q % 2 == 0 else dv(b, a)

    def share(q, half_of):
        cols = pl.ds(pl.multiple_of(half_of * HW + q * QC, QC), QC)
        left = jnp.concatenate([gu[sj(q, a, b)] for b in range(4) for a in range(4)], axis=0)
        return mmt(left[:, 0:FB], wg[cols, :]) + mmt(left[:, FB : 2 * FB], wu[cols, :])

    def sum_send(q):
        val = share(q, c).reshape(16, 32, QC)
        rc(pgo.at[q], sbuf.at[q], ss0, rs0.at[q], sib).wait_recv()

        def at(a, b):
            return val[b * 4 + a] + sbuf[q, a * 4 + b].astype(F32)

        for a in range(4):
            far[q, a] = at(a, 2).astype(BF)
        if q == NQ - 1:
            go(far.at[q], last_in, ss1, rs1.at[2 * q], sdv(q, 0, 2))
            for h, b in ((0, 1), (1, 3)):
                for a in range(4):
                    last_near[h, a] = at(a, b).astype(BF)
                go(last_near.at[h], r1.at[q, h], ss1, rs1.at[2 * q + 1], sdv(q, 0, b))
            for a in range(4):
                own1[q, a] = at(a, 0)
            return
        for h, b in ((0, 1), (1, 3)):
            go(far.at[q, 2 * h : 2 * h + 2], far_in.at[q, h], ss1, rs1.at[2 * q], sdv(q, 0, b))
        for h, b in ((0, 1), (1, 3)):
            for a in range(2):
                near[q, h, a] = at(2 - 2 * h + a, b).astype(BF)
                kept[q, h, a] = at(2 * h + a, b)
            go(near.at[q, h], r1.at[q, h, 2 - 2 * h : 4 - 2 * h], ss1, rs1.at[2 * q + 1], sdv(q, 0, b))
        for a in range(4):
            own1[q, a] = at(a, 0)

    def join(q):
        came(far_in.at[q], rs1.at[2 * q])
        for h, b in ((0, 1), (1, 3)):
            joined[q, h] = (kept[q, h] + far_in[q, h].astype(F32)).astype(BF)
            go(joined.at[q, h], r1.at[q, h, 2 * h : 2 * h + 2], ss1, rs1.at[2 * q + 1], sdv(q, 0, b))

    def second(q):
        last = q == NQ - 1
        if last:
            came(last_in, rs1.at[2 * q])
        came(r1.at[q], rs1.at[2 * q + 1])
        for a in (2, 1, 3, 0):
            s = own1[q, a] + r1[q, 0, a].astype(F32) + r1[q, 1, a].astype(F32)
            if last:
                s = s + last_in[a].astype(F32)
            if a:
                acc1[q, a - 1] = s.astype(BF)
                go(acc1.at[q, a - 1], r2.at[q, a - 1], ss2, rs2.at[q], sdv(q, a, 0))
            else:
                own2[q] = s

    def third(q):
        came(r2.at[q], rs2.at[q])
        own2[q] = own2[q] + r2[q, 0].astype(F32) + r2[q, 1].astype(F32) + r2[q, 2].astype(F32)
        for i in range(16):
            zs[q // 2, i, :, q % 2 * QC : q % 2 * QC + QC] = own2[q, 2 * i : 2 * i + 2, :].astype(BF)

    def line_send(t):
        for i in order:
            dd, cc = zoff[i]
            go(zs.at[t, zz[dd] * 2 + core[cc]], r3.at[t, z, c], ss3.at[t], rs3.at[t], dz(dd, cc))
        r3[t, z, c] = zs[t, me]

    def line_sum(t):
        came(zs.at[t, 0:15], rs3.at[t])
        for h in range(2):
            s = r3[t, 0, h].astype(F32)
            for k in range(1, 8):
                s = s + r3[t, k, h].astype(F32)
            out[:, h * HW + t * HW // 2 : h * HW + (t + 1) * HW // 2] = s.astype(BF)

    def other_half(q):
        pgo[q] = share(q, c0).astype(BF).reshape(16, 32, QC)
        go(pgo.at[q], sbuf.at[q], ss0, rs0.at[q], sib)

    other_half(0)
    other_half(1)
    sum_send(0)
    other_half(2)
    sum_send(1)
    other_half(3)
    join(0)
    sum_send(2)
    join(1)
    sum_send(3)
    hst[...] = hs[...].reshape(512, FB).astype(F32).T.astype(BF)
    join(2)
    weight_grads(0)
    second(0)
    weight_grads(1)
    second(1)
    weight_grads(2)
    second(2)
    weight_grads(3)
    third(0)
    third(1)
    line_send(0)
    second(3)
    weight_grads(4)
    third(2)
    third(3)
    line_send(1)
    weight_grads(5)
    weight_grads(6)
    weight_grads(7)
    line_sum(0)
    line_sum(1)
    for t, (lo, hi) in enumerate(line):
        sent(zbuf.at[0:15, :, lo:hi], s1.at[t])
        sent(zs.at[t, 0:15], ss3.at[t])
    sent(big.at[c, 0:15, :, mycol], sp)
    for g, (lo, hi) in enumerate(SEG):
        sent(big.at[c, 0:15, :, lo:hi], sa.at[g])
    sent(big.at[c, :, :, 0 : 7 * SL], sz)
    sent(big.at[c], ssib)
    sent(pgo, ss0)
    sent(pgo.at[0:3], ss1)
    sent(pgo.at[0, 0:12], ss2)
    for n, (a, b) in enumerate(((dwg, dwg_hbm), (dwu, dwu_hbm), (dwd, dwd_hbm))):
        pltpu.make_async_copy(a, b.at[0], osem.at[n]).wait()


def main_call(*args):
    dma = pltpu.SemaphoreType.DMA
    V = pltpu.VMEM
    vm = pl.BlockSpec(memory_space=V)
    hbm = pl.BlockSpec(memory_space=pl.ANY)
    return pl.pallas_call(
        main_kernel,
        out_shape=(
            jax.ShapeDtypeStruct((2, D), BF),
            jax.ShapeDtypeStruct((1, D, FB), BF),
            jax.ShapeDtypeStruct((1, D, FB), BF),
            jax.ShapeDtypeStruct((1, FB, D), BF),
        ),
        in_specs=[hbm] * 7,
        out_specs=(vm, hbm, hbm, hbm),
        scratch_shapes=[
            V((2, 2), jnp.int32), V((2, 2), F32), V((2, 16, 32, W), BF), V((2, 2, W), BF), V((16, 2, W), BF), V((32, W), F32),
            V((D, FB), BF), V((D, FB), BF), V((FB, D), BF),
            V((3, 3, 16, 32, FB), F32),
            V((16, 32, 2 * FB), BF), V((16, 32, FB), BF), V((FB, 512), BF),
            V((D, FB), BF), V((D, FB), BF), V((FB, D), BF),
            V((NQ, 16, 32, QC), BF), V((NQ, 16, 32, QC), BF), V((NQ, 4, 32, QC), BF), V((NQ, 2, 2, 32, QC), BF), V((4, 32, QC), BF), V((2, 4, 32, QC), BF),
            V((NQ, 2, 2, 32, QC), BF), V((NQ, 2, 2, 32, QC), F32), V((NQ, 2, 2, 32, QC), BF), V((NQ, 4, 32, QC), F32),
            V((NQ, 2, 4, 32, QC), BF), V((NQ, 3, 32, QC), BF), V((NQ, 3, 32, QC), BF), V((NQ, 32, QC), F32),
            V((2, 16, 2, HW // 2), BF), V((2, 8, 2, 2, HW // 2), BF),
            dma((4,)), dma((3,)), dma((3,)), dma((2,)), dma((2,)), dma, dma, dma((2,)), dma((6,)), dma((16,)), dma((8,)),
            dma, dma((4 * SUB,)), dma((4 * SUB,)), dma, dma((5,)), dma, dma((NQ,)), dma, dma((2 * NQ,)),
            dma, dma((NQ,)), dma((2,)), dma((2,)),
        ],
        compiler_params=pltpu.CompilerParams(
            collective_id=0, has_side_effects=True, vmem_limit_bytes=60 << 20
        ),
        name="gather_compute_sum",
    )(*args)


def copy_kernel(*refs):
    loads, stores = [], []
    for a, b, held in zip(refs[0:4], refs[4:8], refs[8:12]):
        pieces = 8 if a.shape[0] == 1 else 1
        n = a.shape[1] // pieces
        for i in range(pieces):
            at = (slice(None), slice(n * i, n * i + n)) if pieces > 1 else (slice(None), slice(None))
            loads.append(pltpu.make_async_copy(a.at[at], held.at[at], refs[12].at[len(loads)]))
            stores.append(pltpu.make_async_copy(held.at[at], b.at[at], refs[13].at[len(stores)]))
    for cp in loads:
        cp.start()
    for load, cp in zip(loads, stores):
        load.wait()
        cp.start()
    for cp in stores:
        cp.wait()


def per_device(tokens, routes, gates, out_grad, gate_weight, up_weight, down_weight):
    results = main_call(tokens, routes, gates, out_grad, gate_weight, up_weight, down_weight)
    hbm = pl.BlockSpec(memory_space=pl.ANY)
    return pl.pallas_call(
        copy_kernel,
        out_shape=tuple(jax.ShapeDtypeStruct(a.shape, a.dtype) for a in results),
        in_specs=[hbm] * 4,
        out_specs=(hbm,) * 4,
        scratch_shapes=[pltpu.VMEM(a.shape, a.dtype) for a in results] + [pltpu.SemaphoreType.DMA((25,))] * 2,
        name="copy_results",
    )(*results)


def solution(mesh):
    return jax.shard_map(
        per_device,
        mesh=mesh,
        in_specs=(
            P(("expert", "fsdp"), None),
            P(("expert", "fsdp"), None),
            P(("expert", "fsdp"), None),
            P(("expert", "fsdp"), None),
            P("expert", None, "fsdp"),
            P("expert", None, "fsdp"),
            P("expert", "fsdp", None),
        ),
        out_specs=(
            P(("expert", "fsdp"), None),
            P("expert", None, "fsdp"),
            P("expert", None, "fsdp"),
            P("expert", "fsdp", None),
        ),
        check_vma=False,
    )
```
